512 devices in a mesh: seq: 64 (over y, x, core), head: 8 (over z).
Axes of the slice: x: 4, y: 8, z: 8, core: 2. Of those that a mesh axis runs over, the one named last changes fastest.
Arguments:
- ssm_input: bfloat16 [32768, 3072], P('seq', 'head'), may hold values from -125 to 125
- input_map: bfloat16 [32768, 1024], P('seq', 'head'), may hold values from -0.4375 to 0.4375
- output_map: bfloat16 [32768, 1024], P('seq', 'head'), may hold values from -0.4375 to 0.4375
- decay_forward: bfloat16 [48, 32768], P('head', 'seq'), may hold values from -2 to 0
- decay_reverse: bfloat16 [48, 32768], P('head', 'seq'), may hold values from -2 to 0
- skip_gain: float32 [48], P('head'), may hold values from 0.2 to 1
- norm_gain: float32 [3072], P('head'), may hold values from 0.5 to 1.5
- scan_order: int32 [4096], P('seq'), may hold values from 0 to 4095, as said below
- raster_order: int32 [4096], P('seq'), may hold values from 0 to 4095, as said below
- grad_normed: bfloat16 [32768, 3072], P('seq', 'head'), may hold values from -6 to 6
Outputs:
- normed_output: bfloat16 [32768, 3072], P('seq', 'head')
- grad_input: bfloat16 [32768, 3072], P('seq', 'head')
The draws below stay inside these ranges and needn't reach their ends.
Inputs may be any that keep to these rules, and one draw needn't show every extreme that they name: scan_order is a permutation of the units; the units held by any index of seq, as positions 64 * e to 64 * e + 63, come one from every index of seq. raster_order is the inverse of scan_order.
All inputs are finite; a program needn't handle non-finite values.
Results may differ from the reference program's by a relative error of at most 0.011.
Values may be sent and summed in bfloat16 or wider, within the bound.
No kernel may reach another device: no remote copies, remote signals or barrier semaphores. Data moves between devices by JAX's collectives and lax.ppermute only.
A program may use at most 128 MiB of HBM per device.

```python
import math
import jax
import jax.numpy as jnp
from jax import lax

HEAD_TOTAL = 48
HEAD_DIM = 64
STATE = 128
GROUPS = 8
SPAN = 256
TOK_DEV = 512
TOKEN_TOTAL = 32768
UNIT = 8
UNITS_DEV = 64
NUNITS = 4096
FEATURES = 3072


def unit_routes(key):
    first_key, second_key = jax.random.split(key)
    senders = jax.vmap(lambda sub_key: jax.random.permutation(sub_key, UNITS_DEV))(jax.random.split(first_key, UNITS_DEV))
    picks = jax.vmap(lambda sub_key: jax.random.permutation(sub_key, UNITS_DEV))(jax.random.split(second_key, UNITS_DEV))
    dest_grid = jnp.broadcast_to(jnp.arange(UNITS_DEV)[:, None], (UNITS_DEV, UNITS_DEV))
    local_unit = picks[senders, dest_grid]
    return (senders * UNITS_DEV + local_unit).reshape(-1).astype(jnp.int32)


def draw_scan_order(key, part):
    routes = unit_routes(key)
    return routes


def draw_raster_order(key, part):
    routes = unit_routes(key)
    return jnp.argsort(routes).astype(jnp.int32)


def draw_ssm_input(key, part):
    key = jax.random.fold_in(key, 11)
    value_key, head_key, row_key = jax.random.split(key, 3)
    head_scale = jnp.exp(jax.random.uniform(head_key, (HEAD_TOTAL,), minval=math.log(0.5), maxval=math.log(5.0)))
    row_scale = jnp.exp(jax.random.uniform(row_key, (TOKEN_TOTAL,), minval=math.log(0.5), maxval=math.log(5.0)))
    raw_values = jnp.clip(jax.random.normal(value_key, (TOKEN_TOTAL, FEATURES)), -5.0, 5.0)
    column_scale = jnp.repeat(head_scale, HEAD_DIM)
    return (raw_values * column_scale[None, :] * row_scale[:, None]).astype(jnp.bfloat16)


def decay_law(key, fast_share):
    random_key_list = jax.random.split(key, 8)
    block_count = TOKEN_TOTAL // TOK_DEV
    fast_heads = jax.random.randint(random_key_list[0], (HEAD_TOTAL,), 0, 8) < fast_share
    fast_blocks = jax.random.randint(random_key_list[7], (HEAD_TOTAL, block_count), 0, 2) == 0
    fast_mask = jnp.logical_and(fast_heads[:, None], fast_blocks)
    fast_rate = jax.random.uniform(random_key_list[1], (HEAD_TOTAL,), minval=1.0 / 50.0, maxval=1.0 / 30.0)
    slow_rate = jax.random.uniform(random_key_list[2], (HEAD_TOTAL,), minval=0.2, maxval=0.6) * math.log(2.0) / TOKEN_TOTAL
    block_rate = jnp.where(fast_mask, fast_rate[:, None], slow_rate[:, None])
    roughness = jnp.exp(jax.random.uniform(random_key_list[3], (HEAD_TOTAL, TOKEN_TOTAL), minval=-math.log(2.0), maxval=math.log(2.0)))
    block_factor = jnp.exp(jax.random.uniform(random_key_list[4], (block_count,), minval=-math.log(2.0), maxval=math.log(2.0)))
    constant_level = -jnp.repeat(block_rate * block_factor[None, :], TOK_DEV, axis=1) * roughness
    spike_position = jax.random.randint(random_key_list[5], (HEAD_TOTAL, 2), 0, TOKEN_TOTAL)
    spike_length = jnp.log(jax.random.uniform(random_key_list[6], (HEAD_TOTAL, 2), minval=0.5, maxval=0.8))
    head_numbers = jnp.broadcast_to(jnp.arange(HEAD_TOTAL)[:, None], (HEAD_TOTAL, 2))
    spike_list = jnp.zeros((HEAD_TOTAL, TOKEN_TOTAL), jnp.float32).at[head_numbers, spike_position].add(spike_length)
    return (constant_level + spike_list).astype(jnp.bfloat16)


def draw_decay_forward(key, part):
    key = jax.random.fold_in(key, 21)
    return decay_law(key, 4)


def draw_decay_reverse(key, part):
    key = jax.random.fold_in(key, 22)
    return decay_law(key, 4)


def block_levels(rng, dims, shards, least, high):
    gain, own = 1.0, jax.random.fold_in(rng, 6)
    for dim, parts in shards:
        draws = jnp.exp(jax.random.uniform(jax.random.fold_in(own, dim), (parts,), jnp.float32, least / len(shards), high / len(shards)))
        gain = gain * jnp.repeat(draws, dims[dim] // parts).reshape([-1 if axis == dim else 1 for axis in range(len(dims))])
    return gain


def scatter_about(own_key, dims, scale, most, cuts=(), held_as=jnp.bfloat16):
    level = block_levels(own_key, dims, cuts, -0.22, 0.18) if cuts else 1.0
    drawn = jax.random.normal(own_key, dims, jnp.float32) * scale * level
    return jnp.minimum(jnp.maximum(drawn, -most), most).astype(held_as)


def setup_inputs(seed: int = 0) -> dict:
    seeds = jax.random.split(jax.random.key(seed), 11)
    return {
        "ssm_input": draw_ssm_input(jax.random.fold_in(seeds[10], 71), 0),
        "input_map": scatter_about(seeds[1], (TOKEN_TOTAL, GROUPS * STATE), 0.03, 0.4375, ((0, 64), (1, 8))),
        "output_map": scatter_about(seeds[2], (TOKEN_TOTAL, GROUPS * STATE), 0.03, 0.4375, ((0, 64), (1, 8))),
        "decay_forward": draw_decay_forward(jax.random.fold_in(seeds[10], 71), 0),
        "decay_reverse": draw_decay_reverse(jax.random.fold_in(seeds[10], 71), 0),
        "skip_gain": jnp.clip(0.2 + 0.8 * jax.random.uniform(seeds[5], (HEAD_TOTAL,), jnp.float32) ** block_levels(seeds[5], (HEAD_TOTAL,), ((0, 8),), -0.2, 0.2), 0.2, 1.0),
        "norm_gain": jnp.clip(1.0 + 0.1 * jax.random.normal(seeds[6], (FEATURES,), jnp.float32), 0.5, 1.5),
        "scan_order": draw_scan_order(jax.random.fold_in(seeds[10], 71), 0),
        "raster_order": draw_raster_order(jax.random.fold_in(seeds[10], 71), 0),
        "grad_normed": scatter_about(seeds[9], (TOKEN_TOTAL, FEATURES), 1.0, 6.0, ((0, 64), (1, 8))),
    }


EPSILON = 1e-05
HIGHEST = lax.Precision.HIGHEST

def span_update(state_in, pieces, reverse):
    value_span, key_span, query_span, decay_span = pieces
    per_group = HEAD_TOTAL // GROUPS
    cumulative = jnp.cumsum(decay_span.astype(jnp.float32), axis=1)
    key_rows = key_span.astype(jnp.float32)
    query_rows = query_span.astype(jnp.float32)
    values = value_span.astype(jnp.float32)
    scores = jnp.einsum('ign,jgn->gij', query_rows, key_rows, precision=HIGHEST)
    scores = jnp.repeat(scores, per_group, axis=0)
    spread = cumulative[:, :, None] - cumulative[:, None, :]
    row_ids = lax.broadcasted_iota(jnp.int32, (SPAN, SPAN), 0)
    col_ids = lax.broadcasted_iota(jnp.int32, (SPAN, SPAN), 1)
    span_end = cumulative[:, -1]
    if reverse:
        allowed = col_ids >= row_ids
        damping = jnp.exp(jnp.minimum(-spread, 0.0))
        key_weight = jnp.exp(cumulative)
        query_weight = jnp.exp(span_end[:, None] - cumulative)
    else:
        allowed = col_ids <= row_ids
        damping = jnp.exp(jnp.minimum(spread, 0.0))
        key_weight = jnp.exp(span_end[:, None] - cumulative)
        query_weight = jnp.exp(cumulative)
    weights = jnp.where(allowed[None], scores * damping, 0.0)
    weights = lax.optimization_barrier(weights.astype(jnp.bfloat16)).astype(jnp.float32)
    inner_part = jnp.einsum('hij,jhp->ihp', weights, values, precision=HIGHEST)
    head_queries = jnp.repeat(query_rows, per_group, axis=1)
    head_keys = jnp.repeat(key_rows, per_group, axis=1)
    state_bf = lax.optimization_barrier(state_in.astype(jnp.bfloat16)).astype(jnp.float32)
    outer_part = jnp.einsum('ihn,hnp->ihp', head_queries, state_bf, precision=HIGHEST)
    outer_part = outer_part * query_weight.T[:, :, None]
    scaled_keys = head_keys * key_weight.T[:, :, None]
    scaled_keys = lax.optimization_barrier(scaled_keys.astype(jnp.bfloat16)).astype(jnp.float32)
    contrib = jnp.einsum('jhn,jhp->hnp', scaled_keys, values, precision=HIGHEST)
    state_out = jnp.exp(span_end)[:, None, None] * state_in + contrib
    return (state_out, inner_part + outer_part)

def scan_all(values, key_rows, query_rows, log_decay, reverse):
    length = values.shape[0]
    span_count = length // SPAN
    value_spans = values.reshape(span_count, SPAN, HEAD_TOTAL, HEAD_DIM)
    key_spans = key_rows.reshape(span_count, SPAN, GROUPS, STATE)
    query_spans = query_rows.reshape(span_count, SPAN, GROUPS, STATE)
    decay_spans = log_decay.reshape(HEAD_TOTAL, span_count, SPAN).transpose(1, 0, 2)
    start_state = jnp.zeros((HEAD_TOTAL, STATE, HEAD_DIM), jnp.float32)

    def advance(state_in, pieces):
        return span_update(state_in, pieces, reverse)
    _, outputs = lax.scan(advance, start_state, (value_spans, key_spans, query_spans, decay_spans), reverse=reverse)
    return outputs.reshape(length, HEAD_TOTAL * HEAD_DIM)

def to_scan(array, scan_order):
    return array.reshape(NUNITS, UNIT, -1)[scan_order].reshape(array.shape)

def to_raster(array, raster_order):
    return array.reshape(NUNITS, UNIT, -1)[raster_order].reshape(array.shape)

def reference(ssm_input, input_map, output_map, decay_forward, decay_reverse, skip_gain, norm_gain, scan_order, raster_order, grad_normed):
    scan_input = to_scan(ssm_input, scan_order)
    scan_in_map = to_scan(input_map, scan_order)
    scan_out_map = to_scan(output_map, scan_order)
    y_forward = scan_all(ssm_input, input_map, output_map, decay_forward, False).astype(jnp.bfloat16)
    y_reverse_scan = scan_all(scan_input, scan_in_map, scan_out_map, decay_reverse, True).astype(jnp.bfloat16)
    y_reverse = to_raster(y_reverse_scan, raster_order)
    skip_cols = jnp.repeat(skip_gain, HEAD_DIM)
    combined = y_forward.astype(jnp.float32) + y_reverse.astype(jnp.float32) + skip_cols * ssm_input.astype(jnp.float32)
    inv_rms = lax.rsqrt(lax.optimization_barrier(jnp.sum(combined * combined, axis=1)) / FEATURES + EPSILON)
    normed_output = (combined * inv_rms[:, None] * norm_gain).astype(jnp.bfloat16)
    scaled_grad = norm_gain * grad_normed.astype(jnp.float32)
    inner_sum = lax.optimization_barrier(jnp.sum(combined * scaled_grad, axis=1))
    grad_combined = inv_rms[:, None] * scaled_grad - combined * (inv_rms ** 3 * inner_sum / FEATURES)[:, None]
    grad_combined = grad_combined.astype(jnp.bfloat16)
    grad_forward = scan_all(grad_combined, output_map, input_map, decay_forward, True).astype(jnp.bfloat16)
    grad_reverse_scan = scan_all(to_scan(grad_combined, scan_order), scan_out_map, scan_in_map, decay_reverse, False).astype(jnp.bfloat16)
    grad_reverse = to_raster(grad_reverse_scan, raster_order)
    grad_input = grad_forward.astype(jnp.float32) + grad_reverse.astype(jnp.float32) + skip_cols * grad_combined.astype(jnp.float32)
    return (normed_output, grad_input.astype(jnp.bfloat16))
```

```python
import jax
import jax.numpy as jnp
from jax import lax
from jax.experimental import pallas as pl
from jax.experimental.pallas import tpu as pltpu
from jax.sharding import PartitionSpec as P

TOK = 512
UNIT = 8
UNITS = 64
HEADS = 6
WIDTH = 384
STATE = 128
SPAN = 256
FEATURES = 3072
CUT = 96
LANES = 128
EPSILON = 1e-05
F32 = jnp.float32
BF16 = jnp.bfloat16


def dot(a, b, ca=1, cb=0, precision=None):
    return lax.dot_general(
        a, b, (((ca,), (cb,)), ((), ())), precision=precision, preferred_element_type=F32
    )


def iota(shape, dim):
    return lax.broadcasted_iota(jnp.int32, shape, dim)


def indicator(mask, dtype=BF16):
    return jnp.where(mask, 1.0, 0.0).astype(dtype)


def partner_rows(index_ref):
    partner = (index_ref[...] >> 6).astype(F32)
    return jnp.broadcast_to(partner, (16, UNITS)).astype(BF16)


def send_matrix(index_ref):
    repeat = indicator((iota((UNITS, TOK), 1) >> 3) == iota((UNITS, TOK), 0))
    partner = dot(partner_rows(index_ref), repeat)[0:1].astype(jnp.int32)
    target = partner * UNIT + (iota((1, TOK), 1) & 7)
    return indicator(iota((TOK, TOK), 0) == target)


def receive_matrix(index_ref):
    repeat = indicator((iota((TOK, UNITS), 0) >> 3) == iota((TOK, UNITS), 1))
    partner = dot(repeat, partner_rows(index_ref), 1, 1)[:, 0:1].astype(jnp.int32)
    source = partner * UNIT + (iota((TOK, 1), 0) & 7)
    return indicator(iota((TOK, TOK), 1) == source)


def padded_decay(decay_ref):
    decay = decay_ref[...].astype(F32)
    return jnp.concatenate([decay, jnp.zeros((16 - HEADS, TOK), F32)], axis=0).astype(BF16)


def lower_ones():
    return indicator(iota((TOK, TOK), 1) <= iota((TOK, TOK), 0))


def running_wide(decay, lower):
    spread = indicator((iota((16, WIDTH), 1) >> 6) == iota((16, WIDTH), 0))
    return dot(lower, dot(decay, spread, 0, 0).astype(BF16))


def cut_state(state):
    state = state.astype(BF16)
    row, col = iota((WIDTH, LANES), 0), iota((WIDTH, LANES), 1)
    parts = [
        dot(state, indicator((row == CUT * part + col) & (col < CUT))) for part in range(WIDTH // CUT)
    ]
    return jnp.concatenate(parts, axis=0)


def join_state(slices):
    row, col = iota((LANES, WIDTH), 0), iota((LANES, WIDTH), 1)
    total = None
    for part in range(WIDTH // CUT):
        place = indicator((col == CUT * part + row) & (row < CUT))
        piece = dot(slices[STATE * part : STATE * (part + 1)], place)
        total = piece if total is None else total + piece
    return total.astype(BF16)


def local_state(keys, values, weight):
    return dot(keys, (values.astype(F32) * weight).astype(BF16), 0, 0)


def three_parts(value):
    high = value.astype(BF16).astype(F32)
    middle = (value - high).astype(BF16).astype(F32)
    return high, middle, value - high - middle


def slice_heads():
    part = lax.axis_index("seq") >> 4
    first = part + (part >> 1)
    return first, first + 1, 64 - 32 * (part & 1)


def link_logs(slices, lane):
    column = iota((TOK, LANES), 1)
    held = jnp.where((column >= lane) & (column < lane + 3), slices.astype(F32), 0.0)
    total = jnp.sum(held, axis=1, keepdims=True)
    first, second, _ = slice_heads()
    earlier = indicator((iota((UNITS, TOK), 1) >> 3) < iota((UNITS, TOK), 0), F32)
    result = []
    for head in (first, second):
        own = jnp.where((iota((TOK, 1), 0) & 7) == head, total, 0.0)
        past = jnp.where((iota((TOK, UNITS), 0) >> 3) > iota((TOK, UNITS), 1), own, 0.0)
        logs = dot(earlier, past, precision=lax.Precision.HIGHEST)
        before = iota((UNITS, UNITS), 1) < iota((UNITS, UNITS), 0)
        result.append(jnp.where(before, jnp.exp(jnp.minimum(logs, 0.0)), 0.0).astype(BF16))
    return result


def expand_links(links, causal):
    unit = indicator((iota((TOK, UNITS), 0) >> 3) == iota((TOK, UNITS), 1))
    same = (iota((TOK, TOK), 0) & 7) == (iota((TOK, TOK), 1) & 7)
    half = dot(unit, links, 1, 0 if causal else 1).astype(BF16)
    return jnp.where(same, dot(half, unit, 1, 1), 0.0).astype(BF16)


def carry(first, second, slices):
    lane = iota((TOK, LANES), 1)
    _, _, border = slice_heads()
    mixed = jnp.where(lane < border, dot(first, slices), dot(second, slices))
    return jnp.where(lane < CUT, mixed, 0.0)


def span_rows(index):
    return slice(SPAN * index, SPAN * (index + 1))


def build_inner(rows_ref, cols_ref, decay, lower, inner_ref):
    down = dot(lower, decay, 1, 1)
    across = dot(decay, lower, 1, 1)
    allowed = iota((SPAN, SPAN), 1) <= iota((SPAN, SPAN), 0)
    for index in range(TOK // SPAN):
        span = span_rows(index)
        scores = jnp.where(allowed, dot(rows_ref[span, :], cols_ref[span, :], 1, 1), 0.0)
        for head in range(HEADS):
            spread = down[span, head : head + 1] - across[head : head + 1, span]
            weight = scores * jnp.exp(jnp.minimum(spread, 0.0))
            inner_ref[index, head] = weight.astype(BF16)


def apply_inner(inner_ref, values_ref, keys_ref, queries_ref, running, causal, out_ref):
    lane = iota((SPAN, LANES), 1)
    border = running[SPAN - 1 : SPAN]
    source, target = (0, 1) if causal else (1, 0)
    sign = 1.0 if causal else -1.0
    near = jnp.exp(sign * (border - running[span_rows(source)]))
    state = local_state(keys_ref[span_rows(source), :], values_ref[span_rows(source), :], near)
    far = jnp.exp(sign * (running[span_rows(target)] - border))
    crossing = far * dot(queries_ref[span_rows(target), :], state.astype(BF16))
    side = 1 if causal else 0
    for index in range(TOK // SPAN):
        span = span_rows(index)
        for pair in range(HEADS // 2):
            cols = slice(LANES * pair, LANES * (pair + 1))
            block = values_ref[span, cols]
            nothing = jnp.zeros_like(block)
            total = dot(inner_ref[index, 2 * pair], jnp.where(lane < 64, block, nothing), side, 0)
            total += dot(
                inner_ref[index, 2 * pair + 1], jnp.where(lane < 64, nothing, block), side, 0
            )
            if index == target:
                total += crossing[:, cols]
            out_ref[span, cols] = total


def open_raster(x, in_map, out_map, decay_f, decay_r, grad, route, pay):
    send = send_matrix(route)
    pay[:, 0:384] = dot(send, x[...]).astype(BF16)
    pay[:, 384:512] = dot(send, in_map[...]).astype(BF16)
    pay[:, 512:640] = dot(send, out_map[...]).astype(BF16)
    pay[:, 640:1024] = dot(send, grad[...]).astype(BF16)
    running = running_wide(padded_decay(decay_f), lower_ones())
    state = local_state(in_map[...], x[...], jnp.exp(running[TOK - 1 : TOK] - running))
    lane = iota((UNIT, LANES), 1)
    note = jnp.zeros((UNIT, LANES), F32)
    for place, decay_ref in ((CUT, decay_f), (CUT + 3, decay_r)):
        decay = jnp.concatenate([decay_ref[...].astype(F32), jnp.zeros((2, TOK), F32)], axis=0)
        for offset, part in enumerate(three_parts(jnp.sum(decay, axis=1, keepdims=True))):
            note = jnp.where(lane == place + offset, part, note)
    note = jnp.broadcast_to(note[None], (UNITS, UNIT, LANES)).reshape(TOK, LANES)
    pay[:, 1024:1152] = (cut_state(state) + note).astype(BF16)


def inner_raster(x, in_map, out_map, decay_f, decay_r, inner, local, run_f, run_r):
    lower = lower_ones()
    decay = padded_decay(decay_f)
    running = running_wide(decay, lower)
    run_f[...] = running
    run_r[...] = running_wide(padded_decay(decay_r), lower)
    build_inner(out_map, in_map, decay, lower, inner)
    apply_inner(inner, x, in_map, out_map, running, True, local)


def open_scan(got, run_r, route, x, in_map, out_map, grad, pay):
    take = receive_matrix(route)
    x[...] = dot(take, got[:, 0:384]).astype(BF16)
    in_map[...] = dot(take, got[:, 384:512]).astype(BF16)
    out_map[...] = dot(take, got[:, 512:640]).astype(BF16)
    grad[...] = dot(take, got[:, 640:1024]).astype(BF16)
    slices = got[:, 1024:1152]
    first, second = [expand_links(links, True) for links in link_logs(slices, CUT)]
    pay[:, 0:128] = carry(first, second, slices).astype(BF16)
    state = local_state(in_map[...], x[...], jnp.exp(run_r[...]))
    pay[:, 128:256] = cut_state(state).astype(BF16)


def inner_scan(got, x, in_map, out_map, decay_r, run_r, inner, local, links):
    lower = lower_ones()
    build_inner(in_map, out_map, padded_decay(decay_r), lower, inner)
    apply_inner(inner, x, in_map, out_map, run_r[...], False, local)
    slices = got[:, 1024:1152]
    for place, pair in enumerate(link_logs(slices, CUT + 3)):
        links[place] = expand_links(pair, False)
        links[2 + place] = expand_links(pair, True)
    for place, pair in enumerate(link_logs(slices, CUT)):
        links[4 + place] = expand_links(pair, False)


def finish_raster(got, out_map, local, run_f, links, route, y, pay):
    entering = join_state(got[:, 0:128])
    value = local[...] + jnp.exp(run_f[...]) * dot(out_map[...], entering)
    y[...] = value.astype(BF16)
    pay[:, 384:512] = carry(links[0], links[1], got[:, 128:256]).astype(BF16)
    pay[:, 0:384] = dot(send_matrix(route), y[...]).astype(BF16)


def finish_scan(got, out_map, local, run_r, x, grad, skip, gain, route, y, combined, stats):
    entering = join_state(got[:, 384:512])
    weight = jnp.exp(run_r[TOK - 1 : TOK, :] - run_r[...])
    y[...] = (local[...] + weight * dot(out_map[...], entering)).astype(BF16)
    y_forward = dot(receive_matrix(route), got[:, 0:384])
    total = y_forward + y[...].astype(F32) + skip[...] * x[...].astype(F32)
    combined[...] = total
    scaled = gain[...] * grad[...].astype(F32)
    ones = jnp.ones((16, WIDTH), F32)
    squares = dot(ones, total * total, 1, 1, lax.Precision.HIGHEST)[0:1]
    inner = dot(ones, total * scaled, 1, 1, lax.Precision.HIGHEST)[0:1]
    rows = [row[:, LANES * k : LANES * (k + 1)] for row in (squares, inner) for k in range(4)]
    tile = jnp.concatenate(rows, axis=0)
    stats[...] = jnp.broadcast_to(tile[None], (8, 8, LANES)).reshape(64, LANES)


def gradient(combined, scaled, scale, pull):
    return (scale * scaled - combined * pull).astype(BF16)


def open_back(stats, combined, y, out_map, grad, gain, run_r, route, back, pay):
    tile = jnp.sum(stats[...].reshape(8, 8, LANES), axis=0)
    squares = jnp.concatenate([tile[k : k + 1] for k in range(4)], axis=1)
    inner = jnp.concatenate([tile[k : k + 1] for k in range(4, 8)], axis=1)
    scale = lax.rsqrt(squares / FEATURES + EPSILON)
    pull = scale * scale * scale * inner / FEATURES
    parts = [*three_parts(scale), *three_parts(pull), jnp.zeros((10, TOK), F32)]
    parts = jnp.concatenate(parts, axis=0).astype(BF16)
    row, col = iota((16, 2 * WIDTH), 0), iota((16, 2 * WIDTH), 1)
    both = indicator(((row < 3) & (col < WIDTH)) | ((row >= 3) & (row < 6) & (col >= WIDTH)))
    wide = dot(parts, both, 0, 0)
    scaled = gain[...] * grad[...].astype(F32)
    back[...] = gradient(combined[...], scaled, wide[:, 0:WIDTH], wide[:, WIDTH:])
    running = run_r[...]
    state = local_state(out_map[...], back[...], jnp.exp(running[TOK - 1 : TOK] - running))
    send = send_matrix(route)
    pay[:, 0:384] = dot(send, y[...]).astype(BF16)
    lanes = indicator(iota((16, LANES), 1) == CUT + iota((16, LANES), 0))
    note = dot(send, dot(parts, lanes, 0, 0).astype(BF16))
    pay[:, 384:512] = (cut_state(state) + note).astype(BF16)


def inner_back_scan(inner, back, in_map, out_map, run_r, local):
    apply_inner(inner, back, out_map, in_map, run_r[...], True, local)


def middle_raster(
    got, y_forward, x, out_map, grad, skip, gain, run_f, links, route, normed, back, pay
):
    take = receive_matrix(route)
    y_reverse = dot(take, got[:, 0:384])
    slices = got[:, 384:512]
    notes = dot(take, slices).astype(BF16)
    row, col = iota((LANES, 2 * WIDTH), 0) - CUT, iota((LANES, 2 * WIDTH), 1)
    both = indicator(
        ((row >= 0) & (row < 3) & (col < WIDTH)) | ((row >= 3) & (row < 6) & (col >= WIDTH))
    )
    wide = dot(notes, both)
    combined = y_forward[...].astype(F32) + y_reverse + skip[...] * x[...].astype(F32)
    scale = wide[:, 0:WIDTH]
    normed[...] = (combined * scale * gain[...]).astype(BF16)
    scaled = gain[...] * grad[...].astype(F32)
    back[...] = gradient(combined, scaled, scale, wide[:, WIDTH:])
    state = local_state(out_map[...], back[...], jnp.exp(run_f[...]))
    pay[:, 0:128] = carry(links[2], links[3], slices).astype(BF16)
    pay[:, 128:256] = cut_state(state).astype(BF16)


def inner_back_raster(inner, back, in_map, out_map, run_f, local):
    apply_inner(inner, back, out_map, in_map, run_f[...], False, local)


def finish_back_scan(got, in_map, local, run_r, links, route, pay):
    entering = join_state(got[:, 0:128])
    value = (local[...] + jnp.exp(run_r[...]) * dot(in_map[...], entering)).astype(BF16)
    pay[:, 384:512] = carry(links[4], links[5], got[:, 128:256]).astype(BF16)
    pay[:, 0:384] = dot(send_matrix(route), value).astype(BF16)


def finish_back_raster(got, in_map, local, run_f, back, skip, route, out):
    entering = join_state(got[:, 384:512])
    weight = jnp.exp(run_f[TOK - 1 : TOK, :] - run_f[...])
    grad_forward = (local[...] + weight * dot(in_map[...], entering)).astype(BF16).astype(F32)
    grad_reverse = dot(receive_matrix(route), got[:, 0:384])
    total = grad_forward + grad_reverse + skip[...] * back[...].astype(F32)
    out[...] = total.astype(BF16)


def kernel(body, outs, *operands, flops=400_000_000):
    shapes = [jax.ShapeDtypeStruct(shape, dtype) for shape, dtype in outs]
    size = sum(a.size * a.dtype.itemsize for a in (*operands, *shapes))
    return pl.pallas_call(
        body,
        out_shape=shapes,
        compiler_params=pltpu.CompilerParams(vmem_limit_bytes=40 * 2**20),
        cost_estimate=pl.CostEstimate(flops=flops, bytes_accessed=size, transcendentals=0),
        name=body.__name__,
    )(*operands)


def exchange(pay):
    return lax.all_to_all(pay, "seq", split_axis=0, concat_axis=0, tiled=True)


def shards(
    ssm_input,
    input_map,
    output_map,
    decay_forward,
    decay_reverse,
    skip_gain,
    norm_gain,
    scan_order,
    raster_order,
    grad_normed,
):
    to_scan = raster_order.reshape(1, UNITS)
    to_raster = scan_order.reshape(1, UNITS)
    skip = jnp.repeat(skip_gain, WIDTH // HEADS).reshape(1, WIDTH)
    gain = norm_gain.reshape(1, WIDTH)
    wide16, wide32 = ((TOK, WIDTH), BF16), ((TOK, WIDTH), F32)
    rows16 = ((TOK, STATE), BF16)
    inner16 = ((TOK // SPAN, HEADS, SPAN, SPAN), BF16)

    def pay(lanes):
        return ((TOK, lanes), BF16)

    (pay1,) = kernel(
        open_raster, [pay(1152)],
        ssm_input, input_map, output_map, decay_forward, decay_reverse, grad_normed, to_scan,
    )
    got1 = exchange(pay1)
    inner_f, local_f, run_f, run_r = kernel(
        inner_raster, [inner16, wide32, wide32, wide32],
        ssm_input, input_map, output_map, decay_forward, decay_reverse, flops=8_000_000_000,
    )
    x_scan, in_scan, out_scan, grad_scan, pay2 = kernel(
        open_scan, [wide16, rows16, rows16, wide16, pay(256)], got1, run_r, to_raster
    )
    got2 = exchange(pay2)
    inner_r, local_r, links = kernel(
        inner_scan, [inner16, wide32, ((6, TOK, TOK), BF16)],
        got1, x_scan, in_scan, out_scan, decay_reverse, run_r, flops=8_000_000_000,
    )
    y_forward, pay3 = kernel(
        finish_raster, [wide16, pay(512)], got2, output_map, local_f, run_f, links, to_scan
    )
    got3 = exchange(pay3)
    y_scan, combined, stats = kernel(
        finish_scan, [wide16, wide32, ((64, LANES), F32)],
        got3, out_scan, local_r, run_r, x_scan, grad_scan, skip, gain, to_raster,
    )
    all_stats = lax.all_to_all(stats, "head", split_axis=0, concat_axis=0, tiled=True)
    back_scan, pay4 = kernel(
        open_back, [wide16, pay(512)],
        all_stats, combined, y_scan, out_scan, grad_scan, gain, run_r, to_raster,
    )
    got4 = exchange(pay4)
    (local_br,) = kernel(
        inner_back_scan, [wide32], inner_r, back_scan, in_scan, out_scan, run_r,
        flops=4_000_000_000,
    )
    normed, back, pay5 = kernel(
        middle_raster, [wide16, wide16, pay(256)],
        got4, y_forward, ssm_input, output_map, grad_normed, skip, gain, run_f, links, to_scan,
    )
    got5 = exchange(pay5)
    (local_bf,) = kernel(
        inner_back_raster, [wide32], inner_f, back, input_map, output_map, run_f,
        flops=4_000_000_000,
    )
    (pay6,) = kernel(
        finish_back_scan, [pay(512)], got5, in_scan, local_br, run_r, links, to_raster
    )
    got6 = exchange(pay6)
    (grad_input,) = kernel(
        finish_back_raster, [wide16], got6, input_map, local_bf, run_f, back, skip, to_scan
    )
    return normed, grad_input


def solution(mesh):
    return jax.shard_map(
        shards,
        mesh=mesh,
        in_specs=(
            P("seq", "head"),
            P("seq", "head"),
            P("seq", "head"),
            P("head", "seq"),
            P("head", "seq"),
            P("head"),
            P("head"),
            P("seq"),
            P("seq"),
            P("seq", "head"),
        ),
        out_specs=(P("seq", "head"), P("seq", "head")),
        check_vma=False,
    )
```

```python
import jax
import jax.numpy as jnp
from jax import lax
from jax.experimental import pallas as pl
from jax.experimental.pallas import tpu as pltpu
from jax.sharding import PartitionSpec as P

TOK = 512
UNIT = 8
UNITS = 64
HEADS = 6
WIDTH = 384
STATE = 128
SPAN = 256
FEATURES = 3072
CUT = 96
LANES = 128
EPSILON = 1e-05
F32 = jnp.float32
BF16 = jnp.bfloat16


def dot(a, b, ca=1, cb=0, precision=None):
    return lax.dot_general(
        a, b, (((ca,), (cb,)), ((), ())), precision=precision, preferred_element_type=F32
    )


def iota(shape, dim):
    return lax.broadcasted_iota(jnp.int32, shape, dim)


def indicator(mask, dtype=BF16):
    return jnp.where(mask, 1.0, 0.0).astype(dtype)


def partner_row(route, unit):
    return pl.ds(pl.multiple_of((route[0, unit] >> 6) * UNIT, UNIT), UNIT)


BAND = 128
ALL = slice(0, TOK)
BANDS = [slice(BAND * k, BAND * (k + 1)) for k in range(TOK // BAND)]


def put_band(stage, route, rows, values, first=0):
    for unit in range(rows.start // UNIT, rows.stop // UNIT):
        target, place = partner_row(route, unit), UNIT * unit - rows.start
        for plane in range(values.shape[1] // LANES):
            cols = slice(LANES * plane, LANES * (plane + 1))
            stage[first + plane, target, :] = values[place : place + UNIT, cols]


def sent(stage, planes, rows=slice(0, TOK)):
    return jnp.concatenate([stage[plane, rows, :] for plane in range(planes)], axis=1)


def fill(stage, values):
    for plane in range(values.shape[1] // LANES):
        stage[plane] = values[:, LANES * plane : LANES * (plane + 1)].astype(F32)


def own_band(stage, route, rows, planes):
    units = []
    for unit in range(rows.start // UNIT, rows.stop // UNIT):
        source = partner_row(route, unit)
        parts = [stage[plane, source, :] for plane in range(planes)]
        units.append(jnp.concatenate(parts, axis=1))
    return jnp.concatenate(units, axis=0)


def receive_matrix(index_ref):
    partner = jnp.broadcast_to((index_ref[...] >> 6).astype(F32), (16, UNITS)).astype(BF16)
    repeat = indicator((iota((TOK, UNITS), 0) >> 3) == iota((TOK, UNITS), 1))
    partner = dot(repeat, partner, 1, 1)[:, 0:1].astype(jnp.int32)
    source = partner * UNIT + (iota((TOK, 1), 0) & 7)
    return indicator(iota((TOK, TOK), 1) == source)


def padded_decay(decay_ref):
    decay = decay_ref[...].astype(F32)
    return jnp.concatenate([decay, jnp.zeros((16 - HEADS, TOK), F32)], axis=0).astype(BF16)


def lower_ones():
    return indicator(iota((TOK, TOK), 1) <= iota((TOK, TOK), 0))


def running_of(decay_ref):
    return running_wide(padded_decay(decay_ref), lower_ones())


def running_wide(decay, lower):
    spread = indicator((iota((16, WIDTH), 1) >> 6) == iota((16, WIDTH), 0))
    return dot(lower, dot(decay, spread, 0, 0).astype(BF16))


def rolled(tile, shift):
    return pltpu.roll(tile, shift % LANES, 1)


def cut_state(state):
    low, middle, high = [state[:, LANES * k : LANES * (k + 1)] for k in range(3)]
    lane = iota((STATE, LANES), 1)
    parts = [
        low,
        jnp.where(lane < 32, rolled(low, 32), rolled(middle, 32)),
        jnp.where(lane < 64, rolled(middle, 64), rolled(high, 64)),
        rolled(high, 96),
    ]
    return jnp.concatenate([jnp.where(lane < CUT, part, 0.0) for part in parts], axis=0)


def join_state(slices):
    slices = slices.astype(F32)
    first, second, third, fourth = [slices[STATE * k : STATE * (k + 1)] for k in range(4)]
    lane = iota((STATE, LANES), 1)
    tiles = [
        jnp.where(lane < 96, first, rolled(second, 96)),
        jnp.where(lane < 64, rolled(second, 96), rolled(third, 64)),
        jnp.where(lane < 32, rolled(third, 64), rolled(fourth, 32)),
    ]
    return jnp.concatenate(tiles, axis=1).astype(BF16)


def local_state(keys, values, weight):
    return dot(keys, (values.astype(F32) * weight).astype(BF16), 0, 0)


def three_parts(value):
    high = value.astype(BF16).astype(F32)
    middle = (value - high).astype(BF16).astype(F32)
    return high, middle, value - high - middle


def slice_heads():
    part = lax.axis_index("seq") >> 4
    first = part + (part >> 1)
    return first, first + 1, 64 - 32 * (part & 1)


def link_decays(slices, lane, work):
    column = iota((TOK, LANES), 1)
    held = jnp.where((column >= lane) & (column < lane + 3), slices.astype(F32), 0.0)
    work[0] = jnp.broadcast_to(jnp.sum(held, axis=1, keepdims=True), (TOK, LANES))
    first, second, border = slice_heads()
    wanted = jnp.where(iota((UNITS, LANES), 1) < border, first, second)
    total = jnp.zeros((UNITS, LANES), F32)
    for head in range(HEADS):
        total = jnp.where(wanted == head, work[0, pl.ds(head, UNITS, stride=UNIT), :], total)
    return jnp.exp(total)


def carry(decays, slices, causal):
    slices = jnp.where(iota((TOK, LANES), 1) < CUT, slices.astype(F32), 0.0)
    state = jnp.zeros((UNIT, LANES), F32)
    entering = [state] * UNITS
    for device in range(UNITS) if causal else reversed(range(UNITS)):
        entering[device] = state
        own = slices[UNIT * device : UNIT * (device + 1)]
        state = state * decays[device : device + 1, :] + own
    return jnp.concatenate(entering, axis=0)


def span_rows(index):
    return slice(SPAN * index, SPAN * (index + 1))


def build_inner(rows_ref, cols_ref, decay, lower, inner_ref):
    down = dot(lower, decay, 1, 1)
    across = dot(decay, lower, 1, 1)
    allowed = iota((SPAN, SPAN), 1) <= iota((SPAN, SPAN), 0)
    for index in range(TOK // SPAN):
        span = span_rows(index)
        scores = jnp.where(allowed, dot(rows_ref[span, :], cols_ref[span, :], 1, 1), 0.0)
        for head in range(HEADS):
            spread = down[span, head : head + 1] - across[head : head + 1, span]
            weight = scores * jnp.exp(jnp.minimum(spread, 0.0))
            inner_ref[index, head] = weight.astype(BF16)


def apply_inner(inner_ref, values_ref, keys_ref, queries_ref, running, causal, out_ref):
    lane = iota((SPAN, LANES), 1)
    border = running[SPAN - 1 : SPAN]
    source, target = (0, 1) if causal else (1, 0)
    sign = 1.0 if causal else -1.0
    near = jnp.exp(sign * (border - running[span_rows(source)]))
    state = local_state(keys_ref[span_rows(source), :], values_ref[span_rows(source), :], near)
    far = jnp.exp(sign * (running[span_rows(target)] - border))
    crossing = far * dot(queries_ref[span_rows(target), :], state.astype(BF16))
    side = 1 if causal else 0
    for index in range(TOK // SPAN):
        span = span_rows(index)
        for pair in range(HEADS // 2):
            cols = slice(LANES * pair, LANES * (pair + 1))
            block = values_ref[span, cols]
            nothing = jnp.zeros_like(block)
            total = dot(inner_ref[index, 2 * pair], jnp.where(lane < 64, block, nothing), side, 0)
            total += dot(
                inner_ref[index, 2 * pair + 1], jnp.where(lane < 64, nothing, block), side, 0
            )
            if index == target:
                total += crossing[:, cols]
            out_ref[span, cols] = total


def open_raster(x, in_map, out_map, decay_f, decay_r, grad, route, pay, stage):
    lane = iota((UNIT, LANES), 1)
    note = jnp.zeros((UNIT, LANES), F32)
    for place, decay_ref in ((CUT, decay_f), (CUT + 3, decay_r)):
        decay = jnp.concatenate([decay_ref[...].astype(F32), jnp.zeros((2, TOK), F32)], axis=0)
        for offset, part in enumerate(three_parts(jnp.sum(decay, axis=1, keepdims=True))):
            note = jnp.where(lane == place + offset, part, note)
    note = jnp.broadcast_to(note[None], (UNITS, UNIT, LANES)).reshape(TOK, LANES)
    running = running_of(decay_f)
    start = 0
    for source in (in_map, out_map, x, grad):
        put_band(stage, route, ALL, source[...].astype(F32))
        stop = start + source.held.shape[1]
        pay[:, start:stop] = sent(stage, (stop - start) // LANES).astype(BF16)
        if stop >= 640:
            pay.send(cols=slice(0 if stop == 640 else start, stop))
        start = stop
    state = local_state(in_map[...], x[...], jnp.exp(running[TOK - 1 : TOK] - running))
    pay[:, 1024:1152] = (cut_state(state) + note).astype(BF16)
    pay.send(cols=slice(1024, 1152))


def inner_raster(x, in_map, out_map, decay_f, inner, local):
    lower = lower_ones()
    decay = padded_decay(decay_f)
    build_inner(out_map, in_map, decay, lower, inner)
    apply_inner(inner, x, in_map, out_map, running_wide(decay, lower), True, local)


def open_scan(got, decay_r, route, x, in_map, pay, stage):
    slices = got[:, 1024:1152]
    running = running_of(decay_r)
    pay[:, 0:128] = carry(link_decays(slices, CUT, stage), slices, True).astype(BF16)
    pay.send(cols=slice(0, 128))
    fill(stage, jnp.concatenate([got[:, 256:640], got[:, 0:128]], axis=1))
    for rows in BANDS:
        moved = own_band(stage, route, rows, 4).astype(BF16)
        x[rows, :] = moved[:, 0:384]
        in_map[rows, :] = moved[:, 384:512]
    x.send()
    in_map.send()
    state = local_state(in_map[...], x[...], jnp.exp(running))
    pay[:, 128:256] = cut_state(state).astype(BF16)
    pay.send(cols=slice(128, 256))


def inner_scan(
    got, x, in_map, decay_r, route, out_map, grad, inner, local, links_f, links_r, work
):
    take = receive_matrix(route)
    out_map[...] = dot(take, got[:, 128:256]).astype(BF16)
    grad[...] = dot(take, got[:, 640:1024]).astype(BF16)
    lower = lower_ones()
    decay = padded_decay(decay_r)
    build_inner(in_map, out_map, decay, lower, inner)
    apply_inner(inner, x, in_map, out_map, running_wide(decay, lower), False, local)
    slices = got[:, 1024:1152]
    for links, lane in ((links_f, CUT), (links_r, CUT + 3)):
        links[...] = link_decays(slices, lane, work)


def finish_raster(got, out_map, local, decay_f, links, route, y, pay, stage):
    running = running_of(decay_f)
    entering = join_state(got[:, 0:128])
    pay[:, 384:512] = carry(links, got[:, 128:256], False).astype(BF16)
    pay.send(cols=slice(384, 512))
    for rows in BANDS:
        value = local[rows, :] + jnp.exp(running[rows]) * dot(out_map[rows, :], entering)
        y[rows, :] = value.astype(BF16)
        put_band(stage, route, rows, value)
    y.send()
    pay[:, 0:384] = sent(stage, 3).astype(BF16)
    pay.send(cols=slice(0, 384))


def finish_scan(
    got, out_map, local, decay_r, x, grad, skip, gain, route, y, combined, stats, stage
):
    entering = join_state(got[:, 384:512])
    running = running_of(decay_r)
    weight = jnp.exp(running[TOK - 1 : TOK, :] - running)
    fill(stage, got[:, 0:384])
    y_forward = own_band(stage, route, ALL, 3)
    y[...] = (local[...] + weight * dot(out_map[...], entering)).astype(BF16)
    y.send()
    total = y_forward + y[...].astype(F32) + skip[...] * x[...].astype(F32)
    combined[...] = total
    combined.send()
    scaled = gain[...] * grad[...].astype(F32)
    squares, inner = token_sums(total * total), token_sums(total * scaled)
    row = iota((UNIT, LANES), 0)
    tile = jnp.zeros((UNIT, LANES), F32)
    for place, sums in ((0, squares), (4, inner)):
        for k in range(4):
            tile = jnp.where(row == place + k, sums[:, LANES * k : LANES * (k + 1)], tile)
    for place in range(8):
        stats[UNIT * place : UNIT * (place + 1), :] = tile


def token_sums(value):
    folded = value[:, 0:128] + value[:, 128:256] + value[:, 256:384]
    ones = jnp.ones((16, LANES), BF16)
    return sum(dot(ones, part.astype(BF16), 1, 1)[0:1] for part in three_parts(folded)[:2])


def gradient(combined, scaled, scale, pull):
    return (scale * scaled - combined * pull).astype(BF16)


def open_back(stats, combined, y, out_map, grad, gain, decay_r, route, back, pay, stage):
    running = running_of(decay_r)
    tile = jnp.sum(stats[...].reshape(8, 8, LANES), axis=0)
    squares = jnp.concatenate([tile[k : k + 1] for k in range(4)], axis=1)
    inner = jnp.concatenate([tile[k : k + 1] for k in range(4, 8)], axis=1)
    scale = lax.rsqrt(squares / FEATURES + EPSILON)
    pull = scale * scale * scale * inner / FEATURES
    parts = [*three_parts(scale), *three_parts(pull), jnp.zeros((10, TOK), F32)]
    parts = jnp.concatenate(parts, axis=0).astype(BF16)
    row, col = iota((16, 2 * WIDTH), 0), iota((16, 2 * WIDTH), 1)
    both = indicator(((row < 3) & (col < WIDTH)) | ((row >= 3) & (row < 6) & (col >= WIDTH)))
    lanes = indicator(iota((16, LANES), 1) == CUT + iota((16, LANES), 0))
    wide = dot(parts, both, 0, 0)
    put_band(stage, route, ALL, dot(parts, lanes, 0, 0), 3)
    put_band(stage, route, ALL, y[...].astype(F32))
    pay[:, 0:384] = sent(stage, 3).astype(BF16)
    pay.send(cols=slice(0, 384))
    scaled = gain[...] * grad[...].astype(F32)
    back[...] = gradient(combined[...], scaled, wide[:, 0:WIDTH], wide[:, WIDTH:])
    back.send()
    state = local_state(out_map[...], back[...], jnp.exp(running[TOK - 1 : TOK] - running))
    pay[:, 384:512] = (cut_state(state) + stage[3]).astype(BF16)
    pay.send(cols=slice(384, 512))


def inner_back_scan(inner, back, in_map, out_map, decay_r, local):
    apply_inner(inner, back, out_map, in_map, running_of(decay_r), True, local)


def middle_raster(
    got, y_forward, x, out_map, grad, skip, gain, decay_f, links, route, normed, back, pay, stage
):
    running = running_of(decay_f)
    fill(stage, got[...])
    row, col = iota((LANES, 2 * WIDTH), 0) - CUT, iota((LANES, 2 * WIDTH), 1)
    both = indicator(
        ((row >= 0) & (row < 3) & (col < WIDTH)) | ((row >= 3) & (row < 6) & (col >= WIDTH))
    )
    pay[:, 0:128] = carry(links, got[:, 384:512], True).astype(BF16)
    pay.send(cols=slice(0, 128))
    for rows in BANDS:
        moved = own_band(stage, route, rows, 4)
        wide = dot(moved[:, 384:512].astype(BF16), both)
        scale = wide[:, 0:WIDTH]
        total = y_forward[rows, :].astype(F32) + moved[:, 0:384]
        total += skip[...] * x[rows, :].astype(F32)
        normed[rows, :] = (total * scale * gain[...]).astype(BF16)
        scaled = gain[...] * grad[rows, :].astype(F32)
        back[rows, :] = gradient(total, scaled, scale, wide[:, WIDTH:])
    normed.send()
    back.send()
    state = local_state(out_map[...], back[...], jnp.exp(running))
    pay[:, 128:256] = cut_state(state).astype(BF16)
    pay.send(cols=slice(128, 256))


def inner_back_raster(inner, back, in_map, out_map, decay_f, skip, local):
    apply_inner(inner, back, out_map, in_map, running_of(decay_f), False, local)
    local[...] += skip[...] * back[...].astype(F32)


def finish_back_scan(got, in_map, local, decay_r, links, route, pay, stage):
    running = running_of(decay_r)
    entering = join_state(got[:, 0:128])
    pay[:, 384:512] = carry(links, got[:, 128:256], False).astype(BF16)
    pay.send(cols=slice(384, 512))
    for rows in BANDS:
        value = local[rows, :] + jnp.exp(running[rows]) * dot(in_map[rows, :], entering)
        put_band(stage, route, rows, value)
    pay[:, 0:384] = sent(stage, 3).astype(BF16)
    pay.send(cols=slice(0, 384))


def finish_back_raster(got, in_map, local, decay_f, route, out, stage):
    entering = join_state(got[:, 384:512])
    running = running_of(decay_f)
    last = running[TOK - 1 : TOK, :]
    fill(stage, got[:, 0:384])
    for rows in BANDS:
        carried = jnp.exp(last - running[rows]) * dot(in_map[rows, :], entering)
        total = local[rows, :] + carried + own_band(stage, route, rows, 3)
        out[rows, :] = total.astype(BF16)
        out.send(rows)


class Arriving:
    def __init__(self, source, held, semaphore):
        self.held = held
        self.copy = pltpu.make_async_copy(source, held, semaphore)
        self.copy.start()

    def land(self):
        if self.copy is not None:
            self.copy.wait()
            self.copy = None

    def __getitem__(self, index):
        self.land()
        return self.held[index]


class Leaving:
    def __init__(self, held, target, semaphores):
        self.held, self.target, self.semaphores, self.copies = held, target, semaphores, []

    def __setitem__(self, index, value):
        self.held[index] = value

    def __getitem__(self, index):
        return self.held[index]

    def send(self, rows=None, cols=None):
        held, target = self.held, self.target
        if rows is not None or cols is not None:
            index = (rows or slice(0, TOK), cols or slice(0, held.shape[1]))
            held, target = held.at[index], target.at[index]
        copy = pltpu.make_async_copy(held, target, self.semaphores.at[len(self.copies)])
        copy.start()
        self.copies.append(copy)

    def finish(self):
        if not self.copies:
            self.send()
        for copy in self.copies:
            copy.wait()


def whole_kernel(body, outs, *operands, flops, work=False):
    shapes = [jax.ShapeDtypeStruct(shape, dtype) for shape, dtype in outs]
    size = sum(a.size * a.dtype.itemsize for a in (*operands, *shapes))
    return pl.pallas_call(
        body,
        out_shape=shapes,
        scratch_shapes=[pltpu.VMEM((1, TOK, LANES), F32)] * work,
        compiler_params=pltpu.CompilerParams(vmem_limit_bytes=60 * 2**20),
        cost_estimate=pl.CostEstimate(flops=flops, bytes_accessed=size, transcendentals=0),
        name=body.__name__,
    )(*operands)


def kernel(body, outs, *operands, arrived=0, stage=0, flops=400_000_000):
    shapes = [jax.ShapeDtypeStruct(*out[:2]) for out in outs]
    size = sum(a.size * a.dtype.itemsize for a in (*operands, *shapes))
    count = len(operands)
    own = [
        place >= arrived and (not arrived or a.dtype == jnp.int32 or a.size > 5_000)
        for place, a in enumerate(operands)
    ]

    def wrapped(*refs):
        sources, targets = refs[:count], refs[count : count + len(outs)]
        scratch = iter(refs[count + len(outs) :])
        held = [(next(scratch), next(scratch)) if mine else None for mine in own]
        given = list(sources)
        for place in sorted(range(count), key=lambda k: operands[k].size):
            if own[place]:
                given[place] = Arriving(sources[place], *held[place])
        results = [Leaving(next(scratch), target, next(scratch)) for target in targets]
        body(*given, *results, *([next(scratch)] if stage else []))
        for operand in given:
            if isinstance(operand, Arriving):
                operand.land()
        for result in results:
            result.finish()

    scratch_shapes = []
    for operand, mine in zip(operands, own, strict=True):
        if mine:
            space = pltpu.SMEM if operand.dtype == jnp.int32 else pltpu.VMEM
            scratch_shapes += [space(operand.shape, operand.dtype), pltpu.SemaphoreType.DMA]
    for shape, dtype, *sends in outs:
        scratch_shapes += [pltpu.VMEM(shape, dtype), pltpu.SemaphoreType.DMA((*sends, 1)[:1])]
    if stage:
        scratch_shapes.append(pltpu.VMEM((stage // LANES, TOK, LANES), F32))
    whole = pl.BlockSpec(memory_space=pltpu.VMEM)
    apart = pl.BlockSpec(memory_space=pl.ANY)
    operands = [
        pltpu.with_memory_space_constraint(a, pltpu.HBM) if mine else a
        for a, mine in zip(operands, own, strict=True)
    ]
    return pl.pallas_call(
        wrapped,
        out_shape=[pltpu.HBM(*out[:2]) for out in outs],
        in_specs=[apart if mine else whole for mine in own],
        out_specs=[apart] * len(outs),
        scratch_shapes=scratch_shapes,
        compiler_params=pltpu.CompilerParams(vmem_limit_bytes=48 * 2**20),
        cost_estimate=pl.CostEstimate(flops=flops, bytes_accessed=size, transcendentals=0),
        name=body.__name__,
    )(*operands)


def exchange(pay):
    return lax.all_to_all(pay, "seq", split_axis=0, concat_axis=0, tiled=True)


def shards(
    ssm_input,
    input_map,
    output_map,
    decay_forward,
    decay_reverse,
    skip_gain,
    norm_gain,
    scan_order,
    raster_order,
    grad_normed,
):
    to_scan = raster_order.reshape(1, UNITS)
    to_raster = scan_order.reshape(1, UNITS)
    skip = jnp.repeat(skip_gain, WIDTH // HEADS).reshape(1, WIDTH)
    gain = norm_gain.reshape(1, WIDTH)
    wide16, wide32 = ((TOK, WIDTH), BF16), ((TOK, WIDTH), F32)
    rows16 = ((TOK, STATE), BF16)
    inner16 = ((TOK // SPAN, HEADS, SPAN, SPAN), BF16)

    def pay(lanes, sends=2):
        return ((TOK, lanes), BF16, sends)

    (pay1,) = kernel(
        open_raster, [pay(1152, 3)],
        ssm_input, input_map, output_map, decay_forward, decay_reverse, grad_normed, to_scan,
        stage=384,
    )
    got1 = exchange(pay1)
    inner_f, local_f = whole_kernel(
        inner_raster, [inner16, wide32],
        ssm_input, input_map, output_map, decay_forward, flops=8_000_000_000,
    )
    x_scan, in_scan, pay2 = kernel(
        open_scan, [wide16, rows16, pay(256)],
        got1, decay_reverse, to_raster, arrived=1, stage=512,
    )
    got2 = exchange(pay2)
    links32 = ((UNITS, LANES), F32)
    out_scan, grad_scan, inner_r, local_r, links_f, links_r = whole_kernel(
        inner_scan, [rows16, wide16, inner16, wide32, links32, links32],
        got1, x_scan, in_scan, decay_reverse, to_raster, flops=8_000_000_000, work=True,
    )
    y_forward, pay3 = kernel(
        finish_raster, [wide16, pay(512)],
        got2, output_map, local_f, decay_forward, links_r, to_scan, arrived=1, stage=384,
    )
    got3 = exchange(pay3)
    y_scan, combined, stats = kernel(
        finish_scan, [wide16, wide32, ((64, LANES), F32)],
        got3, out_scan, local_r, decay_reverse, x_scan, grad_scan, skip, gain, to_raster, arrived=1, stage=384,
    )
    all_stats = lax.all_to_all(stats, "head", split_axis=0, concat_axis=0, tiled=True)
    back_scan, pay4 = kernel(
        open_back, [wide16, pay(512)],
        all_stats, combined, y_scan, out_scan, grad_scan, gain, decay_reverse, to_raster, arrived=1, stage=512,
    )
    got4 = exchange(pay4)
    (local_br,) = whole_kernel(
        inner_back_scan, [wide32], inner_r, back_scan, in_scan, out_scan, decay_reverse,
        flops=4_000_000_000,
    )
    normed, back, pay5 = kernel(
        middle_raster, [wide16, wide16, pay(256)],
        got4, y_forward, ssm_input, output_map, grad_normed, skip, gain, decay_forward, links_r,
        to_scan, arrived=1, stage=512,
    )
    got5 = exchange(pay5)
    (local_bf,) = whole_kernel(
        inner_back_raster, [wide32], inner_f, back, input_map, output_map, decay_forward, skip,
        flops=4_000_000_000,
    )
    (pay6,) = kernel(
        finish_back_scan, [pay(512)],
        got5, in_scan, local_br, decay_reverse, links_f, to_raster, arrived=1, stage=384,
    )
    got6 = exchange(pay6)
    (grad_input,) = kernel(
        finish_back_raster, [(*wide16, 4)],
        got6, input_map, local_bf, decay_forward, to_scan, arrived=1, stage=384,
    )
    return normed, grad_input


def solution(mesh):
    return jax.shard_map(
        shards,
        mesh=mesh,
        in_specs=(
            P("seq", "head"),
            P("seq", "head"),
            P("seq", "head"),
            P("head", "seq"),
            P("head", "seq"),
            P("head"),
            P("head"),
            P("seq"),
            P("seq"),
            P("seq", "head"),
        ),
        out_specs=(P("seq", "head"), P("seq", "head")),
        check_vma=False,
    )
```

```python
import jax
import jax.numpy as jnp
from jax import lax
from jax.experimental import pallas as pl
from jax.experimental.pallas import tpu as pltpu
from jax.sharding import PartitionSpec as P

TOK = 512
UNIT = 8
UNITS = 64
HEADS = 6
WIDTH = 384
STATE = 128
SPAN = 256
FEATURES = 3072
CUT = 96
LANES = 128
EPSILON = 1e-05
F32 = jnp.float32
BF16 = jnp.bfloat16


def dot(a, b, ca=1, cb=0, precision=None):
    return lax.dot_general(
        a, b, (((ca,), (cb,)), ((), ())), precision=precision, preferred_element_type=F32
    )


def iota(shape, dim):
    return lax.broadcasted_iota(jnp.int32, shape, dim)


def indicator(mask, dtype=BF16):
    return jnp.where(mask, 1.0, 0.0).astype(dtype)


def partner_row(route, unit):
    return pl.ds(pl.multiple_of((route[0, unit] >> 6) * UNIT, UNIT), UNIT)


BAND = 128
ALL = slice(0, TOK)
BANDS = [slice(BAND * k, BAND * (k + 1)) for k in range(TOK // BAND)]


def put_band(stage, route, rows, values, first=0):
    for unit in range(rows.start // UNIT, rows.stop // UNIT):
        target, place = partner_row(route, unit), UNIT * unit - rows.start
        for plane in range(values.shape[1] // LANES):
            cols = slice(LANES * plane, LANES * (plane + 1))
            stage[first + plane, target, :] = values[place : place + UNIT, cols]


def sent(stage, planes, rows=slice(0, TOK)):
    return jnp.concatenate([stage[plane, rows, :] for plane in range(planes)], axis=1)


def fill(stage, values):
    for plane in range(values.shape[1] // LANES):
        stage[plane] = values[:, LANES * plane : LANES * (plane + 1)].astype(F32)


def own_band(stage, route, rows, planes):
    units = []
    for unit in range(rows.start // UNIT, rows.stop // UNIT):
        source = partner_row(route, unit)
        parts = [stage[plane, source, :] for plane in range(planes)]
        units.append(jnp.concatenate(parts, axis=1))
    return jnp.concatenate(units, axis=0)


def receive_matrix(index_ref):
    partner = jnp.broadcast_to((index_ref[...] >> 6).astype(F32), (16, UNITS)).astype(BF16)
    repeat = indicator((iota((TOK, UNITS), 0) >> 3) == iota((TOK, UNITS), 1))
    partner = dot(repeat, partner, 1, 1)[:, 0:1].astype(jnp.int32)
    source = partner * UNIT + (iota((TOK, 1), 0) & 7)
    return indicator(iota((TOK, TOK), 1) == source)


def padded_decay(decay_ref):
    decay = decay_ref[...].astype(F32)
    return jnp.concatenate([decay, jnp.zeros((16 - HEADS, TOK), F32)], axis=0).astype(BF16)


def lower_ones():
    return indicator(iota((TOK, TOK), 1) <= iota((TOK, TOK), 0))


def running_of(decay_ref):
    return running_wide(padded_decay(decay_ref), lower_ones())


def running_wide(decay, lower):
    spread = indicator((iota((16, WIDTH), 1) >> 6) == iota((16, WIDTH), 0))
    return dot(lower, dot(decay, spread, 0, 0).astype(BF16))


def rolled(tile, shift):
    return pltpu.roll(tile, shift % LANES, 1)


def cut_state(state):
    low, middle, high = [state[:, LANES * k : LANES * (k + 1)] for k in range(3)]
    lane = iota((STATE, LANES), 1)
    parts = [
        low,
        jnp.where(lane < 32, rolled(low, 32), rolled(middle, 32)),
        jnp.where(lane < 64, rolled(middle, 64), rolled(high, 64)),
        rolled(high, 96),
    ]
    return jnp.concatenate([jnp.where(lane < CUT, part, 0.0) for part in parts], axis=0)


def join_state(slices):
    slices = slices.astype(F32)
    first, second, third, fourth = [slices[STATE * k : STATE * (k + 1)] for k in range(4)]
    lane = iota((STATE, LANES), 1)
    tiles = [
        jnp.where(lane < 96, first, rolled(second, 96)),
        jnp.where(lane < 64, rolled(second, 96), rolled(third, 64)),
        jnp.where(lane < 32, rolled(third, 64), rolled(fourth, 32)),
    ]
    return jnp.concatenate(tiles, axis=1).astype(BF16)


def local_state(keys, values, weight):
    return dot(keys, (values.astype(F32) * weight).astype(BF16), 0, 0)


def three_parts(value):
    high = value.astype(BF16).astype(F32)
    middle = (value - high).astype(BF16).astype(F32)
    return high, middle, value - high - middle


def slice_heads():
    part = lax.axis_index("seq") >> 4
    first = part + (part >> 1)
    return first, first + 1, 64 - 32 * (part & 1)


def link_decays(slices, lane, work):
    column = iota((TOK, LANES), 1)
    held = jnp.where((column >= lane) & (column < lane + 3), slices.astype(F32), 0.0)
    work[0] = jnp.broadcast_to(jnp.sum(held, axis=1, keepdims=True), (TOK, LANES))
    first, second, border = slice_heads()
    wanted = jnp.where(iota((UNITS, LANES), 1) < border, first, second)
    total = jnp.zeros((UNITS, LANES), F32)
    for head in range(HEADS):
        total = jnp.where(wanted == head, work[0, pl.ds(head, UNITS, stride=UNIT), :], total)
    return jnp.exp(total)


def carry(decays, slices, causal):
    slices = jnp.where(iota((TOK, LANES), 1) < CUT, slices.astype(F32), 0.0)
    state = jnp.zeros((UNIT, LANES), F32)
    entering = [state] * UNITS
    for device in range(UNITS) if causal else reversed(range(UNITS)):
        entering[device] = state
        own = slices[UNIT * device : UNIT * (device + 1)]
        state = state * decays[device : device + 1, :] + own
    return jnp.concatenate(entering, axis=0)


def span_rows(index):
    return slice(SPAN * index, SPAN * (index + 1))


def build_inner(rows_ref, cols_ref, decay, lower, inner_ref):
    down = dot(lower, decay, 1, 1)
    across = dot(decay, lower, 1, 1)
    allowed = iota((SPAN, SPAN), 1) <= iota((SPAN, SPAN), 0)
    for index in range(TOK // SPAN):
        span = span_rows(index)
        scores = jnp.where(allowed, dot(rows_ref[span, :], cols_ref[span, :], 1, 1), 0.0)
        for head in range(HEADS):
            spread = down[span, head : head + 1] - across[head : head + 1, span]
            weight = scores * jnp.exp(jnp.minimum(spread, 0.0))
            inner_ref[index, head] = weight.astype(BF16)


def apply_inner(inner_ref, values_ref, keys_ref, queries_ref, running, causal, out_ref):
    lane = iota((SPAN, LANES), 1)
    border = running[SPAN - 1 : SPAN]
    source, target = (0, 1) if causal else (1, 0)
    sign = 1.0 if causal else -1.0
    near = jnp.exp(sign * (border - running[span_rows(source)]))
    state = local_state(keys_ref[span_rows(source), :], values_ref[span_rows(source), :], near)
    far = jnp.exp(sign * (running[span_rows(target)] - border))
    crossing = far * dot(queries_ref[span_rows(target), :], state.astype(BF16))
    side = 1 if causal else 0
    for index in range(TOK // SPAN):
        span = span_rows(index)
        for pair in range(HEADS // 2):
            cols = slice(LANES * pair, LANES * (pair + 1))
            block = values_ref[span, cols]
            nothing = jnp.zeros_like(block)
            total = dot(inner_ref[index, 2 * pair], jnp.where(lane < 64, block, nothing), side, 0)
            total += dot(
                inner_ref[index, 2 * pair + 1], jnp.where(lane < 64, nothing, block), side, 0
            )
            if index == target:
                total += crossing[:, cols]
            out_ref[span, cols] = total.astype(out_ref.dtype)


def open_raster(x, in_map, out_map, decay_f, decay_r, grad, route, pay, stage):
    lane = iota((UNIT, LANES), 1)
    note = jnp.zeros((UNIT, LANES), F32)
    for place, decay_ref in ((CUT, decay_f), (CUT + 3, decay_r)):
        decay = jnp.concatenate([decay_ref[...].astype(F32), jnp.zeros((2, TOK), F32)], axis=0)
        for offset, part in enumerate(three_parts(jnp.sum(decay, axis=1, keepdims=True))):
            note = jnp.where(lane == place + offset, part, note)
    note = jnp.broadcast_to(note[None], (UNITS, UNIT, LANES)).reshape(TOK, LANES)
    running = running_of(decay_f)
    start = 0
    for source in (in_map, out_map, x, grad):
        put_band(stage, route, ALL, source[...].astype(F32))
        stop = start + source.held.shape[1]
        pay[:, start:stop] = sent(stage, (stop - start) // LANES).astype(BF16)
        if stop >= 640:
            pay.send(cols=slice(0 if stop == 640 else start, stop))
        start = stop
    state = local_state(in_map[...], x[...], jnp.exp(running[TOK - 1 : TOK] - running))
    pay[:, 1024:1152] = (cut_state(state) + note).astype(BF16)
    pay.send(cols=slice(1024, 1152))


def inner_raster(x, in_map, out_map, decay_f, skip, gain, inner, local):
    lower = lower_ones()
    decay = padded_decay(decay_f)
    build_inner(out_map, in_map, decay, lower, inner)
    apply_inner(inner, x, in_map, out_map, running_wide(decay, lower), True, local)


def open_scan(got, decay_r, route, x, in_map, pay, stage):
    slices = got[:, 1024:1152]
    running = running_of(decay_r)
    pay[:, 0:128] = carry(link_decays(slices, CUT, stage), slices, True).astype(BF16)
    pay.send(cols=slice(0, 128))
    fill(stage, jnp.concatenate([got[:, 256:640], got[:, 0:128]], axis=1))
    for rows in BANDS:
        moved = own_band(stage, route, rows, 4).astype(BF16)
        x[rows, :] = moved[:, 0:384]
        in_map[rows, :] = moved[:, 384:512]
    x.send()
    in_map.send()
    state = local_state(in_map[...], x[...], jnp.exp(running))
    pay[:, 128:256] = cut_state(state).astype(BF16)
    pay.send(cols=slice(128, 256))


def inner_scan(
    got, x, in_map, decay_r, route, out_map, grad, inner, local, links_f, links_r, work
):
    take = receive_matrix(route)
    out_map[...] = dot(take, got[:, 128:256]).astype(BF16)
    grad[...] = dot(take, got[:, 640:1024]).astype(BF16)
    lower = lower_ones()
    decay = padded_decay(decay_r)
    build_inner(in_map, out_map, decay, lower, inner)
    apply_inner(inner, x, in_map, out_map, running_wide(decay, lower), False, local)
    slices = got[:, 1024:1152]
    for links, lane in ((links_f, CUT), (links_r, CUT + 3)):
        links[...] = link_decays(slices, lane, work)


def finish_raster(got, out_map, local, decay_f, links, route, y, pay, stage):
    running = running_of(decay_f)
    entering = join_state(got[:, 0:128])
    pay[:, 384:512] = carry(links, got[:, 128:256], False).astype(BF16)
    for rows in BANDS:
        value = local[rows, :].astype(F32) + jnp.exp(running[rows]) * dot(out_map[rows, :], entering)
        y[rows, :] = value.astype(BF16)
        put_band(stage, route, rows, value)
    y.send()
    pay[:, 0:384] = sent(stage, 3).astype(BF16)


def finish_scan(
    got, out_map, local, decay_r, x, grad, skip, gain, route, y, combined, stats, stage
):
    entering = join_state(got[:, 384:512])
    running = running_of(decay_r)
    weight = jnp.exp(running[TOK - 1 : TOK, :] - running)
    fill(stage, got[:, 0:384])
    y_forward = own_band(stage, route, ALL, 3)
    y[...] = (local[...].astype(F32) + weight * dot(out_map[...], entering)).astype(BF16)
    total = y_forward + y[...].astype(F32) + skip[...] * x[...].astype(F32)
    combined[...] = total
    scaled = gain[...] * grad[...].astype(F32)
    squares, inner = token_sums(total * total), token_sums(total * scaled)
    row = iota((UNIT, LANES), 0)
    tile = jnp.zeros((UNIT, LANES), F32)
    for place, sums in ((0, squares), (4, inner)):
        for k in range(4):
            tile = jnp.where(row == place + k, sums[:, LANES * k : LANES * (k + 1)], tile)
    for place in range(8):
        stats[UNIT * place : UNIT * (place + 1), :] = tile


def token_sums(value):
    folded = value[:, 0:128] + value[:, 128:256] + value[:, 256:384]
    ones = jnp.ones((16, LANES), BF16)
    return sum(dot(ones, part.astype(BF16), 1, 1)[0:1] for part in three_parts(folded)[:2])


def gradient(combined, scaled, scale, pull):
    return (scale * scaled - combined * pull).astype(BF16)


def open_back(stats, combined, y, out_map, grad, gain, decay_r, route, back, pay, stage):
    running = running_of(decay_r)
    tile = jnp.sum(stats[...].reshape(8, 8, LANES), axis=0)
    squares = jnp.concatenate([tile[k : k + 1] for k in range(4)], axis=1)
    inner = jnp.concatenate([tile[k : k + 1] for k in range(4, 8)], axis=1)
    scale = lax.rsqrt(squares / FEATURES + EPSILON)
    pull = scale * scale * scale * inner / FEATURES
    parts = [*three_parts(scale), *three_parts(pull), jnp.zeros((10, TOK), F32)]
    parts = jnp.concatenate(parts, axis=0).astype(BF16)
    row, col = iota((16, 2 * WIDTH), 0), iota((16, 2 * WIDTH), 1)
    both = indicator(((row < 3) & (col < WIDTH)) | ((row >= 3) & (row < 6) & (col >= WIDTH)))
    lanes = indicator(iota((16, LANES), 1) == CUT + iota((16, LANES), 0))
    wide = dot(parts, both, 0, 0)
    put_band(stage, route, ALL, dot(parts, lanes, 0, 0), 3)
    put_band(stage, route, ALL, y[...].astype(F32))
    pay[:, 0:384] = sent(stage, 3).astype(BF16)
    scaled = gain[...] * grad[...].astype(F32)
    back[...] = gradient(combined[...], scaled, wide[:, 0:WIDTH], wide[:, WIDTH:])
    back.send()
    state = local_state(out_map[...], back[...], jnp.exp(running[TOK - 1 : TOK] - running))
    pay[:, 384:512] = (cut_state(state) + stage[3]).astype(BF16)


def inner_back_scan(inner, back, in_map, out_map, decay_r, local):
    apply_inner(inner, back, out_map, in_map, running_of(decay_r), True, local)


def middle_raster(
    got, y_forward, x, out_map, grad, skip, gain, decay_f, links, route, normed, back, pay, stage
):
    running = running_of(decay_f)
    fill(stage, got[...])
    row, col = iota((LANES, 2 * WIDTH), 0) - CUT, iota((LANES, 2 * WIDTH), 1)
    both = indicator(
        ((row >= 0) & (row < 3) & (col < WIDTH)) | ((row >= 3) & (row < 6) & (col >= WIDTH))
    )
    pay[:, 0:128] = carry(links, got[:, 384:512], True).astype(BF16)
    pay.send(cols=slice(0, 128))
    for rows in BANDS:
        moved = own_band(stage, route, rows, 4)
        wide = dot(moved[:, 384:512].astype(BF16), both)
        scale = wide[:, 0:WIDTH]
        total = y_forward[rows, :].astype(F32) + moved[:, 0:384]
        total += skip[...] * x[rows, :].astype(F32)
        normed[rows, :] = (total * scale * gain[...]).astype(BF16)
        scaled = gain[...] * grad[rows, :].astype(F32)
        back[rows, :] = gradient(total, scaled, scale, wide[:, WIDTH:])
    normed.send()
    back.send()
    state = local_state(out_map[...], back[...], jnp.exp(running))
    pay[:, 128:256] = cut_state(state).astype(BF16)
    pay.send(cols=slice(128, 256))


def inner_back_raster(inner, back, in_map, out_map, decay_f, skip, local):
    apply_inner(inner, back, out_map, in_map, running_of(decay_f), False, local)
    local[...] = (local[...].astype(F32) + skip[...] * back[...].astype(F32)).astype(BF16)


def finish_back_scan(got, in_map, local, decay_r, links, route, pay, stage):
    running = running_of(decay_r)
    entering = join_state(got[:, 0:128])
    pay[:, 384:512] = carry(links, got[:, 128:256], False).astype(BF16)
    pay.send(cols=slice(384, 512))
    for rows in BANDS:
        value = local[rows, :].astype(F32) + jnp.exp(running[rows]) * dot(in_map[rows, :], entering)
        put_band(stage, route, rows, value)
    pay[:, 0:384] = sent(stage, 3).astype(BF16)
    pay.send(cols=slice(0, 384))


def finish_back_raster(got, in_map, local, decay_f, route, out, stage):
    entering = join_state(got[:, 384:512])
    running = running_of(decay_f)
    last = running[TOK - 1 : TOK, :]
    fill(stage, got[:, 0:384])
    for rows in BANDS:
        carried = jnp.exp(last - running[rows]) * dot(in_map[rows, :], entering)
        total = local[rows, :].astype(F32) + carried + own_band(stage, route, rows, 3)
        out[rows, :] = total.astype(BF16)
        out.send(rows)


class Arriving:
    def __init__(self, source, held, semaphore):
        self.held = held
        self.copy = pltpu.make_async_copy(source, held, semaphore)
        self.copy.start()

    def land(self):
        if self.copy is not None:
            self.copy.wait()
            self.copy = None

    def __getitem__(self, index):
        self.land()
        return self.held[index]


class Leaving:
    def __init__(self, held, target, semaphores):
        self.held, self.target, self.semaphores, self.copies = held, target, semaphores, []

    def __setitem__(self, index, value):
        self.held[index] = value

    def __getitem__(self, index):
        return self.held[index]

    def send(self, rows=None, cols=None):
        held, target = self.held, self.target
        if rows is not None or cols is not None:
            index = (rows or slice(0, TOK), cols or slice(0, held.shape[1]))
            held, target = held.at[index], target.at[index]
        copy = pltpu.make_async_copy(held, target, self.semaphores.at[len(self.copies)])
        copy.start()
        self.copies.append(copy)

    def finish(self):
        if not self.copies:
            self.send()
        for copy in self.copies:
            copy.wait()


def whole_kernel(body, outs, *operands, flops, work=False):
    shapes = [jax.ShapeDtypeStruct(shape, dtype) for shape, dtype in outs]
    size = sum(a.size * a.dtype.itemsize for a in (*operands, *shapes))
    return pl.pallas_call(
        body,
        out_shape=shapes,
        scratch_shapes=[pltpu.VMEM((1, TOK, LANES), F32)] * work,
        compiler_params=pltpu.CompilerParams(vmem_limit_bytes=60 * 2**20),
        cost_estimate=pl.CostEstimate(flops=flops, bytes_accessed=size, transcendentals=0),
        name=body.__name__,
    )(*operands)


def kernel(body, outs, *operands, arrived=0, stage=0, flops=400_000_000):
    shapes = [jax.ShapeDtypeStruct(*out[:2]) for out in outs]
    size = sum(a.size * a.dtype.itemsize for a in (*operands, *shapes))
    sends = [(*out, 1)[2] for out in outs]
    count = len(operands)
    own = [
        place >= arrived and (not arrived or a.dtype == jnp.int32 or a.size > 5_000)
        for place, a in enumerate(operands)
    ]

    def wrapped(*refs):
        sources, targets = refs[:count], refs[count : count + len(outs)]
        scratch = iter(refs[count + len(outs) :])
        held = [(next(scratch), next(scratch)) if mine else None for mine in own]
        given = list(sources)
        for place in sorted(range(count), key=lambda k: operands[k].size):
            if own[place]:
                given[place] = Arriving(sources[place], *held[place])
        results = [
            Leaving(next(scratch), target, next(scratch)) if times else target
            for target, times in zip(targets, sends, strict=True)
        ]
        body(*given, *results, *([next(scratch)] if stage else []))
        for operand in given:
            if isinstance(operand, Arriving):
                operand.land()
        for result in results:
            if isinstance(result, Leaving):
                result.finish()

    scratch_shapes = []
    for operand, mine in zip(operands, own, strict=True):
        if mine:
            space = pltpu.SMEM if operand.dtype == jnp.int32 else pltpu.VMEM
            scratch_shapes += [space(operand.shape, operand.dtype), pltpu.SemaphoreType.DMA]
    for shape, times in zip(shapes, sends, strict=True):
        if times:
            scratch_shapes += [pltpu.VMEM(shape.shape, shape.dtype), pltpu.SemaphoreType.DMA((times,))]
    if stage:
        scratch_shapes.append(pltpu.VMEM((stage // LANES, TOK, LANES), F32))
    whole = pl.BlockSpec(memory_space=pltpu.VMEM)
    apart = pl.BlockSpec(memory_space=pl.ANY)
    operands = [
        pltpu.with_memory_space_constraint(a, pltpu.HBM) if mine else a
        for a, mine in zip(operands, own, strict=True)
    ]
    return pl.pallas_call(
        wrapped,
        out_shape=[
            pltpu.HBM(shape.shape, shape.dtype) if times else shape
            for shape, times in zip(shapes, sends, strict=True)
        ],
        in_specs=[apart if mine else whole for mine in own],
        out_specs=[apart if times else whole for times in sends],
        scratch_shapes=scratch_shapes,
        compiler_params=pltpu.CompilerParams(vmem_limit_bytes=48 * 2**20),
        cost_estimate=pl.CostEstimate(flops=flops, bytes_accessed=size, transcendentals=0),
        name=body.__name__,
    )(*operands)


def exchange(pay):
    return lax.all_to_all(pay, "seq", split_axis=0, concat_axis=0, tiled=True)


def shards(
    ssm_input,
    input_map,
    output_map,
    decay_forward,
    decay_reverse,
    skip_gain,
    norm_gain,
    scan_order,
    raster_order,
    grad_normed,
):
    to_scan = raster_order.reshape(1, UNITS)
    to_raster = scan_order.reshape(1, UNITS)
    skip = jnp.repeat(skip_gain, WIDTH // HEADS).reshape(1, WIDTH)
    gain = norm_gain.reshape(1, WIDTH)
    wide16, wide32 = ((TOK, WIDTH), BF16), ((TOK, WIDTH), F32)
    rows16 = ((TOK, STATE), BF16)
    inner16 = ((TOK // SPAN, HEADS, SPAN, SPAN), BF16)

    def pay(lanes, sends=2):
        return ((TOK, lanes), BF16, sends)

    (pay1,) = kernel(
        open_raster, [pay(1152, 3)],
        ssm_input, input_map, output_map, decay_forward, decay_reverse, grad_normed, to_scan,
        stage=384,
    )
    got1 = exchange(pay1)
    inner_f, local_f = whole_kernel(
        inner_raster, [inner16, wide16],
        ssm_input, input_map, output_map, decay_forward, skip, gain, flops=8_000_000_000,
    )
    x_scan, in_scan, pay2 = kernel(
        open_scan, [wide16, rows16, pay(256)],
        got1, decay_reverse, to_raster, arrived=1, stage=512,
    )
    got2 = exchange(pay2)
    links32 = ((UNITS, LANES), F32)
    out_scan, grad_scan, inner_r, local_r, links_f, links_r = whole_kernel(
        inner_scan, [rows16, wide16, inner16, wide16, links32, links32],
        got1, x_scan, in_scan, decay_reverse, to_raster, flops=8_000_000_000, work=True,
    )
    y_forward, pay3 = kernel(
        finish_raster, [wide16, pay(512, 0)],
        got2, output_map, local_f, decay_forward, links_r, to_scan, arrived=1, stage=384,
    )
    got3 = exchange(pay3)
    y_scan, combined, stats = kernel(
        finish_scan, [(*wide16, 0), (*wide32, 0), ((64, LANES), F32, 0)],
        got3, out_scan, local_r, decay_reverse, x_scan, grad_scan, skip, gain, to_raster, arrived=1, stage=384,
    )
    all_stats = lax.all_to_all(stats, "head", split_axis=0, concat_axis=0, tiled=True)
    back_scan, pay4 = kernel(
        open_back, [wide16, pay(512, 0)],
        all_stats, combined, y_scan, out_scan, grad_scan, gain, decay_reverse, to_raster, arrived=3, stage=512,
    )
    got4 = exchange(pay4)
    (local_br,) = whole_kernel(
        inner_back_scan, [wide16], inner_r, back_scan, in_scan, out_scan, decay_reverse,
        flops=4_000_000_000,
    )
    normed, back, pay5 = kernel(
        middle_raster, [wide16, wide16, pay(256)],
        got4, y_forward, ssm_input, output_map, grad_normed, skip, gain, decay_forward, links_r,
        to_scan, arrived=1, stage=512,
    )
    got5 = exchange(pay5)
    (local_bf,) = whole_kernel(
        inner_back_raster, [wide16], inner_f, back, input_map, output_map, decay_forward, skip,
        flops=4_000_000_000,
    )
    (pay6,) = kernel(
        finish_back_scan, [pay(512)],
        got5, in_scan, local_br, decay_reverse, links_f, to_raster, arrived=1, stage=384,
    )
    got6 = exchange(pay6)
    (grad_input,) = kernel(
        finish_back_raster, [(*wide16, 4)],
        got6, input_map, local_bf, decay_forward, to_scan, arrived=1, stage=384,
    )
    return normed, grad_input


def solution(mesh):
    return jax.shard_map(
        shards,
        mesh=mesh,
        in_specs=(
            P("seq", "head"),
            P("seq", "head"),
            P("seq", "head"),
            P("head", "seq"),
            P("head", "seq"),
            P("head"),
            P("head"),
            P("seq"),
            P("seq"),
            P("seq", "head"),
        ),
        out_specs=(P("seq", "head"), P("seq", "head")),
        check_vma=False,
    )
```

```python
import jax
import jax.numpy as jnp
from jax import lax
from jax.experimental import pallas as pl
from jax.experimental.pallas import tpu as pltpu
from jax.sharding import PartitionSpec as P

TOK = 512
UNIT = 8
UNITS = 64
HEADS = 6
WIDTH = 384
STATE = 128
SPAN = 256
FEATURES = 3072
CUT = 96
LANES = 128
EPSILON = 1e-05
F32 = jnp.float32
BF16 = jnp.bfloat16


def dot(a, b, ca=1, cb=0, precision=None):
    return lax.dot_general(
        a, b, (((ca,), (cb,)), ((), ())), precision=precision, preferred_element_type=F32
    )


def iota(shape, dim):
    return lax.broadcasted_iota(jnp.int32, shape, dim)


def indicator(mask, dtype=BF16):
    return jnp.where(mask, 1.0, 0.0).astype(dtype)


def partner_row(route, unit):
    return pl.ds(pl.multiple_of((route[0, unit] >> 6) * UNIT, UNIT), UNIT)


BAND = 128
ALL = slice(0, TOK)
BANDS = [slice(BAND * k, BAND * (k + 1)) for k in range(TOK // BAND)]


def put_band(stage, route, rows, values, first=0):
    for unit in range(rows.start // UNIT, rows.stop // UNIT):
        target, place = partner_row(route, unit), UNIT * unit - rows.start
        for plane in range(values.shape[1] // LANES):
            cols = slice(LANES * plane, LANES * (plane + 1))
            stage[first + plane, target, :] = values[place : place + UNIT, cols]


def sent(stage, planes, rows=slice(0, TOK)):
    return jnp.concatenate([stage[plane, rows, :] for plane in range(planes)], axis=1)


def fill(stage, values):
    for plane in range(values.shape[1] // LANES):
        stage[plane] = values[:, LANES * plane : LANES * (plane + 1)].astype(F32)


def own_band(stage, route, rows, planes):
    units = []
    for unit in range(rows.start // UNIT, rows.stop // UNIT):
        source = partner_row(route, unit)
        parts = [stage[plane, source, :] for plane in range(planes)]
        units.append(jnp.concatenate(parts, axis=1))
    return jnp.concatenate(units, axis=0)


def receive_matrix(index_ref):
    partner = jnp.broadcast_to((index_ref[...] >> 6).astype(F32), (16, UNITS)).astype(BF16)
    repeat = indicator((iota((TOK, UNITS), 0) >> 3) == iota((TOK, UNITS), 1))
    partner = dot(repeat, partner, 1, 1)[:, 0:1].astype(jnp.int32)
    source = partner * UNIT + (iota((TOK, 1), 0) & 7)
    return indicator(iota((TOK, TOK), 1) == source)


def padded_decay(decay_ref):
    decay = decay_ref[...].astype(F32)
    return jnp.concatenate([decay, jnp.zeros((16 - HEADS, TOK), F32)], axis=0).astype(BF16)


def lower_ones():
    return indicator(iota((TOK, TOK), 1) <= iota((TOK, TOK), 0))


def running_of(decay_ref):
    return running_wide(padded_decay(decay_ref), lower_ones())


def running_wide(decay, lower):
    spread = indicator((iota((16, WIDTH), 1) >> 6) == iota((16, WIDTH), 0))
    return dot(lower, dot(decay, spread, 0, 0).astype(BF16))


def rolled(tile, shift):
    return pltpu.roll(tile, shift % LANES, 1)


def cut_state(state):
    low, middle, high = [state[:, LANES * k : LANES * (k + 1)] for k in range(3)]
    lane = iota((STATE, LANES), 1)
    parts = [
        low,
        jnp.where(lane < 32, rolled(low, 32), rolled(middle, 32)),
        jnp.where(lane < 64, rolled(middle, 64), rolled(high, 64)),
        rolled(high, 96),
    ]
    return jnp.concatenate([jnp.where(lane < CUT, part, 0.0) for part in parts], axis=0)


def join_state(slices):
    slices = slices.astype(F32)
    first, second, third, fourth = [slices[STATE * k : STATE * (k + 1)] for k in range(4)]
    lane = iota((STATE, LANES), 1)
    tiles = [
        jnp.where(lane < 96, first, rolled(second, 96)),
        jnp.where(lane < 64, rolled(second, 96), rolled(third, 64)),
        jnp.where(lane < 32, rolled(third, 64), rolled(fourth, 32)),
    ]
    return jnp.concatenate(tiles, axis=1).astype(BF16)


def local_state(keys, values, weight):
    return dot(keys, (values.astype(F32) * weight).astype(BF16), 0, 0)


def three_parts(value):
    high = value.astype(BF16).astype(F32)
    middle = (value - high).astype(BF16).astype(F32)
    return high, middle, value - high - middle


def slice_heads():
    part = lax.axis_index("seq") >> 4
    first = part + (part >> 1)
    return first, first + 1, 64 - 32 * (part & 1)


def link_decays(slices, lane, work):
    column = iota((TOK, LANES), 1)
    held = jnp.where((column >= lane) & (column < lane + 3), slices.astype(F32), 0.0)
    work[0] = jnp.broadcast_to(jnp.sum(held, axis=1, keepdims=True), (TOK, LANES))
    first, second, border = slice_heads()
    wanted = jnp.where(iota((UNITS, LANES), 1) < border, first, second)
    total = jnp.zeros((UNITS, LANES), F32)
    for head in range(HEADS):
        total = jnp.where(wanted == head, work[0, pl.ds(head, UNITS, stride=UNIT), :], total)
    return jnp.exp(total)


def carry(decays, slices, causal):
    slices = jnp.where(iota((TOK, LANES), 1) < CUT, slices.astype(F32), 0.0)
    state = jnp.zeros((UNIT, LANES), F32)
    entering = [state] * UNITS
    for device in range(UNITS) if causal else reversed(range(UNITS)):
        entering[device] = state
        own = slices[UNIT * device : UNIT * (device + 1)]
        state = state * decays[device : device + 1, :] + own
    return jnp.concatenate(entering, axis=0)


def span_rows(index):
    return slice(SPAN * index, SPAN * (index + 1))


def build_inner(rows_ref, cols_ref, decay, lower, inner_ref):
    down = dot(lower, decay, 1, 1)
    across = dot(decay, lower, 1, 1)
    allowed = iota((SPAN, SPAN), 1) <= iota((SPAN, SPAN), 0)
    for index in range(TOK // SPAN):
        span = span_rows(index)
        scores = jnp.where(allowed, dot(rows_ref[span, :], cols_ref[span, :], 1, 1), 0.0)
        for head in range(HEADS):
            spread = down[span, head : head + 1] - across[head : head + 1, span]
            weight = scores * jnp.exp(jnp.minimum(spread, 0.0))
            inner_ref[index, head] = weight.astype(BF16)


def apply_inner(inner_ref, values_ref, keys_ref, queries_ref, running, causal, out_ref):
    lane = iota((SPAN, LANES), 1)
    border = running[SPAN - 1 : SPAN]
    source, target = (0, 1) if causal else (1, 0)
    sign = 1.0 if causal else -1.0
    near = jnp.exp(sign * (border - running[span_rows(source)]))
    state = local_state(keys_ref[span_rows(source), :], values_ref[span_rows(source), :], near)
    far = jnp.exp(sign * (running[span_rows(target)] - border))
    crossing = far * dot(queries_ref[span_rows(target), :], state.astype(BF16))
    side = 1 if causal else 0
    for index in range(TOK // SPAN):
        span = span_rows(index)
        for pair in range(HEADS // 2):
            cols = slice(LANES * pair, LANES * (pair + 1))
            block = values_ref[span, cols]
            nothing = jnp.zeros_like(block)
            total = dot(inner_ref[index, 2 * pair], jnp.where(lane < 64, block, nothing), side, 0)
            total += dot(
                inner_ref[index, 2 * pair + 1], jnp.where(lane < 64, nothing, block), side, 0
            )
            if index == target:
                total += crossing[:, cols]
            out_ref[span, cols] = total.astype(BF16)


def open_raster(x, in_map, out_map, decay_f, decay_r, grad, route, pay, stage):
    lane = iota((UNIT, LANES), 1)
    note = jnp.zeros((UNIT, LANES), F32)
    for place, decay_ref in ((CUT, decay_f), (CUT + 3, decay_r)):
        decay = jnp.concatenate([decay_ref[...].astype(F32), jnp.zeros((2, TOK), F32)], axis=0)
        for offset, part in enumerate(three_parts(jnp.sum(decay, axis=1, keepdims=True))):
            note = jnp.where(lane == place + offset, part, note)
    note = jnp.broadcast_to(note[None], (UNITS, UNIT, LANES)).reshape(TOK, LANES)
    running = running_of(decay_f)
    start = 0
    for source in (in_map, out_map, x, grad):
        put_band(stage, route, ALL, source[...].astype(F32))
        stop = start + source.held.shape[1]
        pay[:, start:stop] = sent(stage, (stop - start) // LANES).astype(BF16)
        if stop >= 640:
            pay.send(cols=slice(0 if stop == 640 else start, stop))
        start = stop
    state = local_state(in_map[...], x[...], jnp.exp(running[TOK - 1 : TOK] - running))
    pay[:, 1024:1152] = (cut_state(state) + note).astype(BF16)
    pay.send(cols=slice(1024, 1152))


def inner_raster(x, in_map, out_map, decay_f, skip, gain, inner, local):
    lower = lower_ones()
    decay = padded_decay(decay_f)
    build_inner(out_map, in_map, decay, lower, inner)
    apply_inner(inner, x, in_map, out_map, running_wide(decay, lower), True, local)


def open_scan(got, decay_r, route, x, in_map, pay, stage):
    slices = got[:, 1024:1152]
    running = running_of(decay_r)
    pay[:, 0:128] = carry(link_decays(slices, CUT, stage), slices, True).astype(BF16)
    pay.send(cols=slice(0, 128))
    fill(stage, jnp.concatenate([got[:, 256:640], got[:, 0:128]], axis=1))
    for rows in BANDS:
        moved = own_band(stage, route, rows, 4).astype(BF16)
        x[rows, :] = moved[:, 0:384]
        in_map[rows, :] = moved[:, 384:512]
    x.send()
    in_map.send()
    state = local_state(in_map[...], x[...], jnp.exp(running))
    pay[:, 128:256] = cut_state(state).astype(BF16)
    pay.send(cols=slice(128, 256))


def inner_scan(
    got, x, in_map, decay_r, route, out_map, grad, inner, local, links_f, links_r, work
):
    take = receive_matrix(route)
    out_map[...] = dot(take, got[:, 128:256]).astype(BF16)
    grad[...] = dot(take, got[:, 640:1024]).astype(BF16)
    lower = lower_ones()
    decay = padded_decay(decay_r)
    build_inner(in_map, out_map, decay, lower, inner)
    apply_inner(inner, x, in_map, out_map, running_wide(decay, lower), False, local)
    slices = got[:, 1024:1152]
    for links, lane in ((links_f, CUT), (links_r, CUT + 3)):
        links[...] = link_decays(slices, lane, work)


def finish_raster(got, out_map, local, decay_f, links, route, y, pay, stage):
    running = running_of(decay_f)
    entering = join_state(got[:, 0:128])
    pay[:, 384:512] = carry(links, got[:, 128:256], False).astype(BF16)
    for rows in BANDS:
        value = local[rows, :].astype(F32) + jnp.exp(running[rows]) * dot(out_map[rows, :], entering)
        y[rows, :] = value.astype(BF16)
        put_band(stage, route, rows, value)
    y.send()
    pay[:, 0:384] = sent(stage, 3).astype(BF16)


def finish_scan(
    got, out_map, local, decay_r, x, grad, skip, gain, route, y, combined, stats, stage
):
    entering = join_state(got[:, 384:512])
    running = running_of(decay_r)
    weight = jnp.exp(running[TOK - 1 : TOK, :] - running)
    fill(stage, got[:, 0:384])
    y_forward = own_band(stage, route, ALL, 3)
    y[...] = (local[...].astype(F32) + weight * dot(out_map[...], entering)).astype(BF16)
    total = y_forward + y[...].astype(F32) + skip[...] * x[...].astype(F32)
    combined[...] = total
    scaled = gain[...] * grad[...].astype(F32)
    squares, inner = token_sums(total * total), token_sums(total * scaled)
    row = iota((UNIT, LANES), 0)
    tile = jnp.zeros((UNIT, LANES), F32)
    for place, sums in ((0, squares), (4, inner)):
        for k in range(4):
            tile = jnp.where(row == place + k, sums[:, LANES * k : LANES * (k + 1)], tile)
    for place in range(8):
        stats[UNIT * place : UNIT * (place + 1), :] = tile


def token_sums(value):
    folded = value[:, 0:128] + value[:, 128:256] + value[:, 256:384]
    ones = jnp.ones((16, LANES), BF16)
    return sum(dot(ones, part.astype(BF16), 1, 1)[0:1] for part in three_parts(folded)[:2])


def gradient(combined, scaled, scale, pull):
    return (scale * scaled - combined * pull).astype(BF16)


def open_back(stats, combined, y, out_map, grad, gain, decay_r, route, back, pay, stage):
    running = running_of(decay_r)
    tile = jnp.sum(stats[...].reshape(8, 8, LANES), axis=0)
    squares = jnp.concatenate([tile[k : k + 1] for k in range(4)], axis=1)
    inner = jnp.concatenate([tile[k : k + 1] for k in range(4, 8)], axis=1)
    scale = lax.rsqrt(squares / FEATURES + EPSILON)
    pull = scale * scale * scale * inner / FEATURES
    parts = [*three_parts(scale), *three_parts(pull), jnp.zeros((10, TOK), F32)]
    parts = jnp.concatenate(parts, axis=0).astype(BF16)
    row, col = iota((16, 2 * WIDTH), 0), iota((16, 2 * WIDTH), 1)
    both = indicator(((row < 3) & (col < WIDTH)) | ((row >= 3) & (row < 6) & (col >= WIDTH)))
    lanes = indicator(iota((16, LANES), 1) == CUT + iota((16, LANES), 0))
    wide = dot(parts, both, 0, 0)
    put_band(stage, route, ALL, dot(parts, lanes, 0, 0), 3)
    put_band(stage, route, ALL, y[...].astype(F32))
    pay[:, 0:384] = sent(stage, 3).astype(BF16)
    scaled = gain[...] * grad[...].astype(F32)
    back[...] = gradient(combined[...], scaled, wide[:, 0:WIDTH], wide[:, WIDTH:])
    back.send()
    state = local_state(out_map[...], back[...], jnp.exp(running[TOK - 1 : TOK] - running))
    pay[:, 384:512] = (cut_state(state) + stage[3]).astype(BF16)


def inner_back_scan(decay_r, inner, back, in_map, out_map, local):
    apply_inner(inner, back, out_map, in_map, running_of(decay_r), True, local)


def middle_raster(
    got, y_forward, x, out_map, grad, skip, gain, decay_f, links, route, normed, back, pay, stage
):
    running = running_of(decay_f)
    fill(stage, got[...])
    row, col = iota((LANES, 2 * WIDTH), 0) - CUT, iota((LANES, 2 * WIDTH), 1)
    both = indicator(
        ((row >= 0) & (row < 3) & (col < WIDTH)) | ((row >= 3) & (row < 6) & (col >= WIDTH))
    )
    pay[:, 0:128] = carry(links, got[:, 384:512], True).astype(BF16)
    pay.send(cols=slice(0, 128))
    for rows in BANDS:
        moved = own_band(stage, route, rows, 4)
        wide = dot(moved[:, 384:512].astype(BF16), both)
        scale = wide[:, 0:WIDTH]
        total = y_forward[rows, :].astype(F32) + moved[:, 0:384]
        total += skip[...] * x[rows, :].astype(F32)
        normed[rows, :] = (total * scale * gain[...]).astype(BF16)
        scaled = gain[...] * grad[rows, :].astype(F32)
        back[rows, :] = gradient(total, scaled, scale, wide[:, WIDTH:])
    normed.send()
    back.send()
    state = local_state(out_map[...], back[...], jnp.exp(running))
    pay[:, 128:256] = cut_state(state).astype(BF16)
    pay.send(cols=slice(128, 256))


def inner_back_raster(decay_f, inner, back, in_map, out_map, skip, local):
    apply_inner(inner, back, out_map, in_map, running_of(decay_f), False, local)
    local[...] = (local[...].astype(F32) + skip[...] * back[...].astype(F32)).astype(BF16)


def finish_back_scan(got, in_map, local, decay_r, links, route, pay, stage):
    running = running_of(decay_r)
    entering = join_state(got[:, 0:128])
    pay[:, 384:512] = carry(links, got[:, 128:256], False).astype(BF16)
    for rows in BANDS:
        value = local[rows, :].astype(F32) + jnp.exp(running[rows]) * dot(in_map[rows, :], entering)
        put_band(stage, route, rows, value)
    pay[:, 0:384] = sent(stage, 3).astype(BF16)


def finish_back_raster(got, in_map, local, decay_f, route, out, stage):
    entering = join_state(got[:, 384:512])
    running = running_of(decay_f)
    last = running[TOK - 1 : TOK, :]
    fill(stage, got[:, 0:384])
    for rows in BANDS:
        carried = jnp.exp(last - running[rows]) * dot(in_map[rows, :], entering)
        total = local[rows, :].astype(F32) + carried + own_band(stage, route, rows, 3)
        out[rows, :] = total.astype(BF16)
        out.send(rows)


class Arriving:
    def __init__(self, source, held, semaphore):
        self.held = held
        self.copy = pltpu.make_async_copy(source, held, semaphore)
        self.copy.start()

    def land(self):
        if self.copy is not None:
            self.copy.wait()
            self.copy = None

    def __getitem__(self, index):
        self.land()
        return self.held[index]


class Leaving:
    def __init__(self, held, target, semaphores):
        self.held, self.target, self.semaphores, self.copies = held, target, semaphores, []

    def __setitem__(self, index, value):
        self.held[index] = value

    def __getitem__(self, index):
        return self.held[index]

    def send(self, rows=None, cols=None):
        held, target = self.held, self.target
        if rows is not None or cols is not None:
            index = (rows or slice(0, TOK), cols or slice(0, held.shape[1]))
            held, target = held.at[index], target.at[index]
        copy = pltpu.make_async_copy(held, target, self.semaphores.at[len(self.copies)])
        copy.start()
        self.copies.append(copy)

    def finish(self):
        if not self.copies:
            self.send()
        for copy in self.copies:
            copy.wait()


def whole_kernel(body, outs, *operands, flops, work=False):
    shapes = [jax.ShapeDtypeStruct(shape, dtype) for shape, dtype in outs]
    size = sum(a.size * a.dtype.itemsize for a in (*operands, *shapes))
    return pl.pallas_call(
        body,
        out_shape=shapes,
        scratch_shapes=[pltpu.VMEM((1, TOK, LANES), F32)] * work,
        compiler_params=pltpu.CompilerParams(vmem_limit_bytes=60 * 2**20),
        cost_estimate=pl.CostEstimate(flops=flops, bytes_accessed=size, transcendentals=0),
        name=body.__name__,
    )(*operands)


def kernel(body, outs, *operands, arrived=0, stage=0, after=(), flops=400_000_000):
    shapes = [jax.ShapeDtypeStruct(*out[:2]) for out in outs]
    size = sum(a.size * a.dtype.itemsize for a in (*operands, *shapes))
    sends = [(*out, 1)[2] for out in outs]
    count = len(operands)
    own = [
        place >= arrived and (not arrived or a.dtype == jnp.int32 or a.size > 5_000)
        for place, a in enumerate(operands)
    ]

    def wrapped(*refs):
        sources, refs = refs[:count], refs[count + len(after) :]
        targets, scratch = refs[: len(outs)], iter(refs[len(outs) :])
        held = [(next(scratch), next(scratch)) if mine else None for mine in own]
        given = list(sources)
        for place in sorted(range(count), key=lambda k: operands[k].size):
            if own[place]:
                given[place] = Arriving(sources[place], *held[place])
        results = [
            Leaving(next(scratch), target, next(scratch)) if times else target
            for target, times in zip(targets, sends, strict=True)
        ]
        body(*given, *results, *([next(scratch)] if stage else []))
        for operand in given:
            if isinstance(operand, Arriving):
                operand.land()
        for result in results:
            if isinstance(result, Leaving):
                result.finish()

    scratch_shapes = []
    for operand, mine in zip(operands, own, strict=True):
        if mine:
            space = pltpu.SMEM if operand.dtype == jnp.int32 else pltpu.VMEM
            scratch_shapes += [space(operand.shape, operand.dtype), pltpu.SemaphoreType.DMA]
    for shape, times in zip(shapes, sends, strict=True):
        if times:
            scratch_shapes += [pltpu.VMEM(shape.shape, shape.dtype), pltpu.SemaphoreType.DMA((times,))]
    if stage:
        scratch_shapes.append(pltpu.VMEM((stage // LANES, TOK, LANES), F32))
    whole = pl.BlockSpec(memory_space=pltpu.VMEM)
    apart = pl.BlockSpec(memory_space=pl.ANY)
    operands = [
        pltpu.with_memory_space_constraint(a, pltpu.HBM) if mine else a
        for a, mine in zip(operands, own, strict=True)
    ]
    return pl.pallas_call(
        wrapped,
        out_shape=[
            pltpu.HBM(shape.shape, shape.dtype) if times else shape
            for shape, times in zip(shapes, sends, strict=True)
        ],
        in_specs=[apart if mine else whole for mine in own] + [apart] * len(after),
        out_specs=[apart if times else whole for times in sends],
        scratch_shapes=scratch_shapes,
        compiler_params=pltpu.CompilerParams(vmem_limit_bytes=48 * 2**20),
        cost_estimate=pl.CostEstimate(flops=flops, bytes_accessed=size, transcendentals=0),
        name=body.__name__,
    )(*operands, *(pltpu.with_memory_space_constraint(a, pltpu.HBM) for a in after))


def exchange(pay):
    return lax.all_to_all(pay, "seq", split_axis=0, concat_axis=0, tiled=True)


def shards(
    ssm_input,
    input_map,
    output_map,
    decay_forward,
    decay_reverse,
    skip_gain,
    norm_gain,
    scan_order,
    raster_order,
    grad_normed,
):
    to_scan = raster_order.reshape(1, UNITS)
    to_raster = scan_order.reshape(1, UNITS)
    skip = jnp.repeat(skip_gain, WIDTH // HEADS).reshape(1, WIDTH)
    gain = norm_gain.reshape(1, WIDTH)
    wide16, wide32 = ((TOK, WIDTH), BF16), ((TOK, WIDTH), F32)
    rows16 = ((TOK, STATE), BF16)
    inner16 = ((TOK // SPAN, HEADS, SPAN, SPAN), BF16)

    def pay(lanes, sends=2):
        return ((TOK, lanes), BF16, sends)

    (pay1,) = kernel(
        open_raster, [pay(1152, 3)],
        ssm_input, input_map, output_map, decay_forward, decay_reverse, grad_normed, to_scan,
        stage=384,
    )
    got1 = exchange(pay1)
    inner_f, local_f = whole_kernel(
        inner_raster, [inner16, wide16],
        ssm_input, input_map, output_map, decay_forward, skip, gain, flops=8_000_000_000,
    )
    x_scan, in_scan, pay2 = kernel(
        open_scan, [wide16, rows16, pay(256)],
        got1, decay_reverse, to_raster, arrived=1, stage=512,
    )
    got2 = exchange(pay2)
    links32 = ((UNITS, LANES), F32)
    out_scan, grad_scan, inner_r, local_r, links_f, links_r = whole_kernel(
        inner_scan, [rows16, wide16, inner16, wide16, links32, links32],
        got1, x_scan, in_scan, decay_reverse, to_raster, flops=8_000_000_000, work=True,
    )
    y_forward, pay3 = kernel(
        finish_raster, [wide16, pay(512, 0)],
        got2, output_map, local_f, decay_forward, links_r, to_scan, arrived=1, stage=384,
    )
    got3 = exchange(pay3)
    y_scan, combined, stats = kernel(
        finish_scan, [(*wide16, 0), (*wide32, 0), ((64, LANES), F32, 0)],
        got3, out_scan, local_r, decay_reverse, x_scan, grad_scan, skip, gain, to_raster, arrived=1, stage=384,
    )
    all_stats = lax.all_to_all(stats, "head", split_axis=0, concat_axis=0, tiled=True)
    back_scan, pay4 = kernel(
        open_back, [wide16, pay(512, 0)],
        all_stats, combined, y_scan, out_scan, grad_scan, gain, decay_reverse, to_raster, arrived=3, stage=512,
    )
    got4 = exchange(pay4)
    (local_br,) = kernel(
        inner_back_scan, [wide16], decay_reverse, inner_r, back_scan, in_scan, out_scan,
        arrived=1, flops=4_000_000_000,
    )
    normed, back, pay5 = kernel(
        middle_raster, [wide16, wide16, pay(256)],
        got4, y_forward, ssm_input, output_map, grad_normed, skip, gain, decay_forward, links_r,
        to_scan, arrived=1, stage=512,
    )
    got5 = exchange(pay5)
    (local_bf,) = kernel(
        inner_back_raster, [wide16],
        decay_forward, inner_f, back, input_map, output_map, skip, arrived=1, flops=4_000_000_000,
    )
    (pay6,) = kernel(
        finish_back_scan, [pay(512, 0)],
        got5, in_scan, local_br, decay_reverse, links_f, to_raster, arrived=1, stage=384,
        after=(local_bf,),
    )
    got6 = exchange(pay6)
    (grad_input,) = kernel(
        finish_back_raster, [(*wide16, 4)],
        got6, input_map, local_bf, decay_forward, to_scan, arrived=1, stage=384,
    )
    return normed, grad_input


def solution(mesh):
    return jax.shard_map(
        shards,
        mesh=mesh,
        in_specs=(
            P("seq", "head"),
            P("seq", "head"),
            P("seq", "head"),
            P("head", "seq"),
            P("head", "seq"),
            P("head"),
            P("head"),
            P("seq"),
            P("seq"),
            P("seq", "head"),
        ),
        out_specs=(P("seq", "head"), P("seq", "head")),
        check_vma=False,
    )
```

```python
import jax
import jax.numpy as jnp
from jax import lax
from jax.experimental import pallas as pl
from jax.experimental.pallas import tpu as pltpu
from jax.sharding import PartitionSpec as P

TOK = 512
UNIT = 8
UNITS = 64
HEADS = 6
WIDTH = 384
STATE = 128
SPAN = 256
FEATURES = 3072
CUT = 96
LANES = 128
EPSILON = 1e-05
F32 = jnp.float32
BF16 = jnp.bfloat16


def dot(a, b, ca=1, cb=0, precision=None):
    return lax.dot_general(
        a, b, (((ca,), (cb,)), ((), ())), precision=precision, preferred_element_type=F32
    )


def iota(shape, dim):
    return lax.broadcasted_iota(jnp.int32, shape, dim)


def indicator(mask, dtype=BF16):
    return jnp.where(mask, 1.0, 0.0).astype(dtype)


def partner_row(route, unit):
    return pl.ds(pl.multiple_of((route[0, unit] >> 6) * UNIT, UNIT), UNIT)


BAND = 128
ALL = slice(0, TOK)
BANDS = [slice(BAND * k, BAND * (k + 1)) for k in range(TOK // BAND)]


def put_band(stage, route, rows, values, first=0):
    for unit in range(rows.start // UNIT, rows.stop // UNIT):
        target, place = partner_row(route, unit), UNIT * unit - rows.start
        for plane in range(values.shape[1] // LANES):
            cols = slice(LANES * plane, LANES * (plane + 1))
            stage[first + plane, target, :] = values[place : place + UNIT, cols]


def sent(stage, planes, rows=slice(0, TOK)):
    return jnp.concatenate([stage[plane, rows, :] for plane in range(planes)], axis=1)


def fill(stage, values):
    for plane in range(values.shape[1] // LANES):
        stage[plane] = values[:, LANES * plane : LANES * (plane + 1)].astype(F32)


def own_band(stage, route, rows, planes):
    units = []
    for unit in range(rows.start // UNIT, rows.stop // UNIT):
        source = partner_row(route, unit)
        parts = [stage[plane, source, :] for plane in range(planes)]
        units.append(jnp.concatenate(parts, axis=1))
    return jnp.concatenate(units, axis=0)


def receive_matrix(index_ref):
    partner = jnp.broadcast_to((index_ref[...] >> 6).astype(F32), (16, UNITS)).astype(BF16)
    repeat = indicator((iota((TOK, UNITS), 0) >> 3) == iota((TOK, UNITS), 1))
    partner = dot(repeat, partner, 1, 1)[:, 0:1].astype(jnp.int32)
    source = partner * UNIT + (iota((TOK, 1), 0) & 7)
    return indicator(iota((TOK, TOK), 1) == source)


def padded_decay(decay_ref):
    decay = decay_ref[...].astype(F32)
    return jnp.concatenate([decay, jnp.zeros((16 - HEADS, TOK), F32)], axis=0).astype(BF16)


def lower_ones():
    return indicator(iota((TOK, TOK), 1) <= iota((TOK, TOK), 0))


def running_of(decay_ref):
    return running_wide(padded_decay(decay_ref), lower_ones())


def running_wide(decay, lower):
    spread = indicator((iota((16, WIDTH), 1) >> 6) == iota((16, WIDTH), 0))
    return dot(lower, dot(decay, spread, 0, 0).astype(BF16))


def rolled(tile, shift):
    return pltpu.roll(tile, shift % LANES, 1)


def cut_state(state):
    low, middle, high = [state[:, LANES * k : LANES * (k + 1)] for k in range(3)]
    lane = iota((STATE, LANES), 1)
    parts = [
        low,
        jnp.where(lane < 32, rolled(low, 32), rolled(middle, 32)),
        jnp.where(lane < 64, rolled(middle, 64), rolled(high, 64)),
        rolled(high, 96),
    ]
    return jnp.concatenate([jnp.where(lane < CUT, part, 0.0) for part in parts], axis=0)


def join_state(slices):
    slices = slices.astype(F32)
    first, second, third, fourth = [slices[STATE * k : STATE * (k + 1)] for k in range(4)]
    lane = iota((STATE, LANES), 1)
    tiles = [
        jnp.where(lane < 96, first, rolled(second, 96)),
        jnp.where(lane < 64, rolled(second, 96), rolled(third, 64)),
        jnp.where(lane < 32, rolled(third, 64), rolled(fourth, 32)),
    ]
    return jnp.concatenate(tiles, axis=1).astype(BF16)


def local_state(keys, values, weight):
    return dot(keys, (values.astype(F32) * weight).astype(BF16), 0, 0)


def three_parts(value):
    high = value.astype(BF16).astype(F32)
    middle = (value - high).astype(BF16).astype(F32)
    return high, middle, value - high - middle


def slice_heads():
    part = lax.axis_index("seq") >> 4
    first = part + (part >> 1)
    return first, first + 1, 64 - 32 * (part & 1)


def link_decays(slices, lane, work):
    column = iota((TOK, LANES), 1)
    held = jnp.where((column >= lane) & (column < lane + 3), slices.astype(F32), 0.0)
    work[0] = jnp.broadcast_to(jnp.sum(held, axis=1, keepdims=True), (TOK, LANES))
    first, second, border = slice_heads()
    wanted = jnp.where(iota((UNITS, LANES), 1) < border, first, second)
    total = jnp.zeros((UNITS, LANES), F32)
    for head in range(HEADS):
        total = jnp.where(wanted == head, work[0, pl.ds(head, UNITS, stride=UNIT), :], total)
    return jnp.exp(total)


def carry(decays, slices, causal):
    slices = jnp.where(iota((TOK, LANES), 1) < CUT, slices.astype(F32), 0.0)
    state = jnp.zeros((UNIT, LANES), F32)
    entering = [state] * UNITS
    for device in range(UNITS) if causal else reversed(range(UNITS)):
        entering[device] = state
        own = slices[UNIT * device : UNIT * (device + 1)]
        state = state * decays[device : device + 1, :] + own
    return jnp.concatenate(entering, axis=0)


def span_rows(index):
    return slice(SPAN * index, SPAN * (index + 1))


def build_inner(rows_ref, cols_ref, decay, lower, inner_ref):
    down = dot(lower, decay, 1, 1)
    across = dot(decay, lower, 1, 1)
    allowed = iota((SPAN, SPAN), 1) <= iota((SPAN, SPAN), 0)
    for index in range(TOK // SPAN):
        span = span_rows(index)
        scores = jnp.where(allowed, dot(rows_ref[span, :], cols_ref[span, :], 1, 1), 0.0)
        for head in range(HEADS):
            spread = down[span, head : head + 1] - across[head : head + 1, span]
            weight = scores * jnp.exp(jnp.minimum(spread, 0.0))
            inner_ref[index, head] = weight.astype(BF16)


def apply_inner(inner_ref, values_ref, keys_ref, queries_ref, running, causal, out_ref):
    lane = iota((SPAN, LANES), 1)
    border = running[SPAN - 1 : SPAN]
    source, target = (0, 1) if causal else (1, 0)
    sign = 1.0 if causal else -1.0
    near = jnp.exp(sign * (border - running[span_rows(source)]))
    state = local_state(keys_ref[span_rows(source), :], values_ref[span_rows(source), :], near)
    far = jnp.exp(sign * (running[span_rows(target)] - border))
    crossing = far * dot(queries_ref[span_rows(target), :], state.astype(BF16))
    side = 1 if causal else 0
    for index in range(TOK // SPAN):
        span = span_rows(index)
        for pair in range(HEADS // 2):
            cols = slice(LANES * pair, LANES * (pair + 1))
            block = values_ref[span, cols]
            nothing = jnp.zeros_like(block)
            total = dot(inner_ref[index, 2 * pair], jnp.where(lane < 64, block, nothing), side, 0)
            total += dot(
                inner_ref[index, 2 * pair + 1], jnp.where(lane < 64, nothing, block), side, 0
            )
            if index == target:
                total += crossing[:, cols]
            out_ref[span, cols] = total.astype(BF16)


def open_raster(x, in_map, out_map, decay_f, decay_r, grad, route, pay, stage):
    lane = iota((UNIT, LANES), 1)
    note = jnp.zeros((UNIT, LANES), F32)
    for place, decay_ref in ((CUT, decay_f), (CUT + 3, decay_r)):
        decay = jnp.concatenate([decay_ref[...].astype(F32), jnp.zeros((2, TOK), F32)], axis=0)
        for offset, part in enumerate(three_parts(jnp.sum(decay, axis=1, keepdims=True))):
            note = jnp.where(lane == place + offset, part, note)
    note = jnp.broadcast_to(note[None], (UNITS, UNIT, LANES)).reshape(TOK, LANES)
    running = running_of(decay_f)
    start = 0
    for source in (in_map, out_map, x, grad):
        put_band(stage, route, ALL, source[...].astype(F32))
        stop = start + source.held.shape[1]
        pay[:, start:stop] = sent(stage, (stop - start) // LANES).astype(BF16)
        if stop >= 640:
            pay.send(cols=slice(0 if stop == 640 else start, stop))
        start = stop
    state = local_state(in_map[...], x[...], jnp.exp(running[TOK - 1 : TOK] - running))
    pay[:, 1024:1152] = (cut_state(state) + note).astype(BF16)
    pay.send(cols=slice(1024, 1152))


def inner_raster(x, in_map, out_map, decay_f, skip, gain, inner, local):
    lower = lower_ones()
    decay = padded_decay(decay_f)
    build_inner(out_map, in_map, decay, lower, inner)
    apply_inner(inner, x, in_map, out_map, running_wide(decay, lower), True, local)


def open_scan(got, decay_r, route, x, in_map, pay, stage):
    slices = got[:, 1024:1152]
    running = running_of(decay_r)
    pay[:, 0:128] = carry(link_decays(slices, CUT, stage), slices, True).astype(BF16)
    pay.send(cols=slice(0, 128))
    fill(stage, jnp.concatenate([got[:, 256:640], got[:, 0:128]], axis=1))
    for rows in BANDS:
        moved = own_band(stage, route, rows, 4).astype(BF16)
        x[rows, :] = moved[:, 0:384]
        in_map[rows, :] = moved[:, 384:512]
    x.send()
    in_map.send()
    state = local_state(in_map[...], x[...], jnp.exp(running))
    pay[:, 128:256] = cut_state(state).astype(BF16)
    pay.send(cols=slice(128, 256))


def inner_scan(
    got, x, in_map, decay_r, route, out_map, grad, inner, local, links_f, links_r, work
):
    take = receive_matrix(route)
    out_map[...] = dot(take, got[:, 128:256]).astype(BF16)
    grad[...] = dot(take, got[:, 640:1024]).astype(BF16)
    lower = lower_ones()
    decay = padded_decay(decay_r)
    build_inner(in_map, out_map, decay, lower, inner)
    apply_inner(inner, x, in_map, out_map, running_wide(decay, lower), False, local)
    slices = got[:, 1024:1152]
    for links, lane in ((links_f, CUT), (links_r, CUT + 3)):
        links[...] = link_decays(slices, lane, work)


def finish_raster(got, out_map, local, decay_f, links, route, pay, stage):
    running = running_of(decay_f)
    entering = join_state(got[:, 0:128])
    pay[:, 384:512] = carry(links, got[:, 128:256], False).astype(BF16)
    for rows in BANDS:
        value = local[rows, :].astype(F32) + jnp.exp(running[rows]) * dot(out_map[rows, :], entering)
        put_band(stage, route, rows, value)
    pay[:, 0:384] = sent(stage, 3).astype(BF16)


def finish_scan(
    got, out_map, local, decay_r, x, grad, skip, gain, route, combined, stats, stage
):
    entering = join_state(got[:, 384:512])
    running = running_of(decay_r)
    weight = jnp.exp(running[TOK - 1 : TOK, :] - running)
    fill(stage, got[:, 0:384])
    y_forward = own_band(stage, route, ALL, 3)
    y_reverse = (local[...].astype(F32) + weight * dot(out_map[...], entering)).astype(BF16)
    total = y_forward + y_reverse.astype(F32) + skip[...] * x[...].astype(F32)
    combined[...] = total
    scaled = gain[...] * grad[...].astype(F32)
    squares, inner = token_sums(total * total), token_sums(total * scaled)
    row = iota((UNIT, LANES), 0)
    tile = jnp.zeros((UNIT, LANES), F32)
    for place, sums in ((0, squares), (4, inner)):
        for k in range(4):
            tile = jnp.where(row == place + k, sums[:, LANES * k : LANES * (k + 1)], tile)
    for place in range(8):
        stats[UNIT * place : UNIT * (place + 1), :] = tile


def token_sums(value):
    folded = value[:, 0:128] + value[:, 128:256] + value[:, 256:384]
    ones = jnp.ones((16, LANES), BF16)
    return sum(dot(ones, part.astype(BF16), 1, 1)[0:1] for part in three_parts(folded)[:2])


def gradient(combined, scaled, scale, pull):
    return (scale * scaled - combined * pull).astype(BF16)


def open_back(stats, combined, out_map, grad, gain, decay_r, route, back, pay, stage):
    running = running_of(decay_r)
    tile = jnp.sum(stats[...].reshape(8, 8, LANES), axis=0)
    squares = jnp.concatenate([tile[k : k + 1] for k in range(4)], axis=1)
    inner = jnp.concatenate([tile[k : k + 1] for k in range(4, 8)], axis=1)
    scale = lax.rsqrt(squares / FEATURES + EPSILON)
    pull = scale * scale * scale * inner / FEATURES
    parts = [*three_parts(scale), *three_parts(pull), jnp.zeros((10, TOK), F32)]
    parts = jnp.concatenate(parts, axis=0).astype(BF16)
    row, col = iota((16, 2 * WIDTH), 0), iota((16, 2 * WIDTH), 1)
    both = indicator(((row < 3) & (col < WIDTH)) | ((row >= 3) & (row < 6) & (col >= WIDTH)))
    lanes = indicator(iota((16, LANES), 1) == CUT + iota((16, LANES), 0))
    wide = dot(parts, both, 0, 0)
    put_band(stage, route, ALL, dot(parts, lanes, 0, 0), 3)
    put_band(stage, route, ALL, combined[...])
    pay[:, 0:384] = sent(stage, 3).astype(BF16)
    scaled = gain[...] * grad[...].astype(F32)
    back[...] = gradient(combined[...], scaled, wide[:, 0:WIDTH], wide[:, WIDTH:])
    back.send()
    state = local_state(out_map[...], back[...], jnp.exp(running[TOK - 1 : TOK] - running))
    pay[:, 384:512] = (cut_state(state) + stage[3]).astype(BF16)


def inner_back_scan(decay_r, inner, back, in_map, out_map, local):
    apply_inner(inner, back, out_map, in_map, running_of(decay_r), True, local)


def middle_raster(
    got, out_map, grad, gain, decay_f, links, route, normed, back, pay, stage
):
    running = running_of(decay_f)
    fill(stage, got[...])
    row, col = iota((LANES, 2 * WIDTH), 0) - CUT, iota((LANES, 2 * WIDTH), 1)
    both = indicator(
        ((row >= 0) & (row < 3) & (col < WIDTH)) | ((row >= 3) & (row < 6) & (col >= WIDTH))
    )
    pay[:, 0:128] = carry(links, got[:, 384:512], True).astype(BF16)
    pay.send(cols=slice(0, 128))
    for rows in BANDS:
        moved = own_band(stage, route, rows, 4)
        wide = dot(moved[:, 384:512].astype(BF16), both)
        scale = wide[:, 0:WIDTH]
        total = moved[:, 0:384]
        normed[rows, :] = (total * scale * gain[...]).astype(BF16)
        scaled = gain[...] * grad[rows, :].astype(F32)
        back[rows, :] = gradient(total, scaled, scale, wide[:, WIDTH:])
    normed.send()
    back.send()
    state = local_state(out_map[...], back[...], jnp.exp(running))
    pay[:, 128:256] = cut_state(state).astype(BF16)
    pay.send(cols=slice(128, 256))


def inner_back_raster(decay_f, inner, back, in_map, out_map, skip, local):
    apply_inner(inner, back, out_map, in_map, running_of(decay_f), False, local)
    local[...] = (local[...].astype(F32) + skip[...] * back[...].astype(F32)).astype(BF16)


def finish_back_scan(got, in_map, local, decay_r, links, route, pay, stage):
    running = running_of(decay_r)
    entering = join_state(got[:, 0:128])
    pay[:, 384:512] = carry(links, got[:, 128:256], False).astype(BF16)
    for rows in BANDS:
        value = local[rows, :].astype(F32) + jnp.exp(running[rows]) * dot(in_map[rows, :], entering)
        put_band(stage, route, rows, value)
    pay[:, 0:384] = sent(stage, 3).astype(BF16)


def finish_back_raster(got, in_map, local, decay_f, route, out, stage):
    entering = join_state(got[:, 384:512])
    running = running_of(decay_f)
    last = running[TOK - 1 : TOK, :]
    fill(stage, got[:, 0:384])
    for rows in BANDS:
        carried = jnp.exp(last - running[rows]) * dot(in_map[rows, :], entering)
        total = local[rows, :].astype(F32) + carried + own_band(stage, route, rows, 3)
        out[rows, :] = total.astype(BF16)
        out.send(rows)


class Arriving:
    def __init__(self, source, held, semaphore):
        self.held = held
        self.copy = pltpu.make_async_copy(source, held, semaphore)
        self.copy.start()

    def land(self):
        if self.copy is not None:
            self.copy.wait()
            self.copy = None

    def __getitem__(self, index):
        self.land()
        return self.held[index]


class Leaving:
    def __init__(self, held, target, semaphores):
        self.held, self.target, self.semaphores, self.copies = held, target, semaphores, []

    def __setitem__(self, index, value):
        self.held[index] = value

    def __getitem__(self, index):
        return self.held[index]

    def send(self, rows=None, cols=None):
        held, target = self.held, self.target
        if rows is not None or cols is not None:
            index = (rows or slice(0, TOK), cols or slice(0, held.shape[1]))
            held, target = held.at[index], target.at[index]
        copy = pltpu.make_async_copy(held, target, self.semaphores.at[len(self.copies)])
        copy.start()
        self.copies.append(copy)

    def finish(self):
        if not self.copies:
            self.send()
        for copy in self.copies:
            copy.wait()


def whole_kernel(body, outs, *operands, flops, work=False):
    shapes = [jax.ShapeDtypeStruct(shape, dtype) for shape, dtype in outs]
    size = sum(a.size * a.dtype.itemsize for a in (*operands, *shapes))
    return pl.pallas_call(
        body,
        out_shape=shapes,
        scratch_shapes=[pltpu.VMEM((1, TOK, LANES), F32)] * work,
        compiler_params=pltpu.CompilerParams(vmem_limit_bytes=60 * 2**20),
        cost_estimate=pl.CostEstimate(flops=flops, bytes_accessed=size, transcendentals=0),
        name=body.__name__,
    )(*operands)


def kernel(body, outs, *operands, arrived=0, stage=0, after=(), flops=400_000_000):
    shapes = [jax.ShapeDtypeStruct(*out[:2]) for out in outs]
    size = sum(a.size * a.dtype.itemsize for a in (*operands, *shapes))
    sends = [(*out, 1)[2] for out in outs]
    count = len(operands)
    own = [
        place >= arrived and (not arrived or a.dtype == jnp.int32 or a.size > 5_000)
        for place, a in enumerate(operands)
    ]

    def wrapped(*refs):
        sources, refs = refs[:count], refs[count + len(after) :]
        targets, scratch = refs[: len(outs)], iter(refs[len(outs) :])
        held = [(next(scratch), next(scratch)) if mine else None for mine in own]
        given = list(sources)
        for place in sorted(range(count), key=lambda k: operands[k].size):
            if own[place]:
                given[place] = Arriving(sources[place], *held[place])
        results = [
            Leaving(next(scratch), target, next(scratch)) if times else target
            for target, times in zip(targets, sends, strict=True)
        ]
        body(*given, *results, *([next(scratch)] if stage else []))
        for operand in given:
            if isinstance(operand, Arriving):
                operand.land()
        for result in results:
            if isinstance(result, Leaving):
                result.finish()

    scratch_shapes = []
    for operand, mine in zip(operands, own, strict=True):
        if mine:
            space = pltpu.SMEM if operand.dtype == jnp.int32 else pltpu.VMEM
            scratch_shapes += [space(operand.shape, operand.dtype), pltpu.SemaphoreType.DMA]
    for shape, times in zip(shapes, sends, strict=True):
        if times:
            scratch_shapes += [pltpu.VMEM(shape.shape, shape.dtype), pltpu.SemaphoreType.DMA((times,))]
    if stage:
        scratch_shapes.append(pltpu.VMEM((stage // LANES, TOK, LANES), F32))
    whole = pl.BlockSpec(memory_space=pltpu.VMEM)
    apart = pl.BlockSpec(memory_space=pl.ANY)
    operands = [
        pltpu.with_memory_space_constraint(a, pltpu.HBM) if mine else a
        for a, mine in zip(operands, own, strict=True)
    ]
    return pl.pallas_call(
        wrapped,
        out_shape=[
            pltpu.HBM(shape.shape, shape.dtype) if times else shape
            for shape, times in zip(shapes, sends, strict=True)
        ],
        in_specs=[apart if mine else whole for mine in own] + [apart] * len(after),
        out_specs=[apart if times else whole for times in sends],
        scratch_shapes=scratch_shapes,
        compiler_params=pltpu.CompilerParams(vmem_limit_bytes=48 * 2**20),
        cost_estimate=pl.CostEstimate(flops=flops, bytes_accessed=size, transcendentals=0),
        name=body.__name__,
    )(*operands, *(pltpu.with_memory_space_constraint(a, pltpu.HBM) for a in after))


def exchange(pay):
    return lax.all_to_all(pay, "seq", split_axis=0, concat_axis=0, tiled=True)


def shards(
    ssm_input,
    input_map,
    output_map,
    decay_forward,
    decay_reverse,
    skip_gain,
    norm_gain,
    scan_order,
    raster_order,
    grad_normed,
):
    to_scan = raster_order.reshape(1, UNITS)
    to_raster = scan_order.reshape(1, UNITS)
    skip = jnp.repeat(skip_gain, WIDTH // HEADS).reshape(1, WIDTH)
    gain = norm_gain.reshape(1, WIDTH)
    wide16, wide32 = ((TOK, WIDTH), BF16), ((TOK, WIDTH), F32)
    rows16 = ((TOK, STATE), BF16)
    inner16 = ((TOK // SPAN, HEADS, SPAN, SPAN), BF16)

    def pay(lanes, sends=2):
        return ((TOK, lanes), BF16, sends)

    (pay1,) = kernel(
        open_raster, [pay(1152, 3)],
        ssm_input, input_map, output_map, decay_forward, decay_reverse, grad_normed, to_scan,
        stage=384,
    )
    got1 = exchange(pay1)
    inner_f, local_f = whole_kernel(
        inner_raster, [inner16, wide16],
        ssm_input, input_map, output_map, decay_forward, skip, gain, flops=8_000_000_000,
    )
    x_scan, in_scan, pay2 = kernel(
        open_scan, [wide16, rows16, pay(256)],
        got1, decay_reverse, to_raster, arrived=1, stage=512,
    )
    got2 = exchange(pay2)
    links32 = ((UNITS, LANES), F32)
    out_scan, grad_scan, inner_r, local_r, links_f, links_r = whole_kernel(
        inner_scan, [rows16, wide16, inner16, wide16, links32, links32],
        got1, x_scan, in_scan, decay_reverse, to_raster, flops=8_000_000_000, work=True,
    )
    (pay3,) = kernel(
        finish_raster, [pay(512, 0)],
        got2, output_map, local_f, decay_forward, links_r, to_scan, arrived=1, stage=384,
    )
    got3 = exchange(pay3)
    combined, stats = kernel(
        finish_scan, [(*wide32, 0), ((64, LANES), F32, 0)],
        got3, out_scan, local_r, decay_reverse, x_scan, grad_scan, skip, gain, to_raster, arrived=1, stage=384,
    )
    all_stats = lax.all_to_all(stats, "head", split_axis=0, concat_axis=0, tiled=True)
    back_scan, pay4 = kernel(
        open_back, [wide16, pay(512, 0)],
        all_stats, combined, out_scan, grad_scan, gain, decay_reverse, to_raster, arrived=2, stage=512,
    )
    got4 = exchange(pay4)
    (local_br,) = kernel(
        inner_back_scan, [wide16], decay_reverse, inner_r, back_scan, in_scan, out_scan,
        arrived=1, flops=4_000_000_000,
    )
    normed, back, pay5 = kernel(
        middle_raster, [wide16, wide16, pay(256)],
        got4, output_map, grad_normed, gain, decay_forward, links_r,
        to_scan, arrived=1, stage=512,
    )
    got5 = exchange(pay5)
    (local_bf,) = kernel(
        inner_back_raster, [wide16],
        decay_forward, inner_f, back, input_map, output_map, skip, arrived=1, flops=4_000_000_000,
    )
    (pay6,) = kernel(
        finish_back_scan, [pay(512, 0)],
        got5, in_scan, local_br, decay_reverse, links_f, to_raster, arrived=1, stage=384,
        after=(local_bf,),
    )
    got6 = exchange(pay6)
    (grad_input,) = kernel(
        finish_back_raster, [(*wide16, 4)],
        got6, input_map, local_bf, decay_forward, to_scan, arrived=1, stage=384,
    )
    return normed, grad_input


def solution(mesh):
    return jax.shard_map(
        shards,
        mesh=mesh,
        in_specs=(
            P("seq", "head"),
            P("seq", "head"),
            P("seq", "head"),
            P("head", "seq"),
            P("head", "seq"),
            P("head"),
            P("head"),
            P("seq"),
            P("seq"),
            P("seq", "head"),
        ),
        out_specs=(P("seq", "head"), P("seq", "head")),
        check_vma=False,
    )
```

```python
import jax
import jax.numpy as jnp
from jax import lax
from jax.experimental import pallas as pl
from jax.experimental.pallas import tpu as pltpu
from jax.sharding import PartitionSpec as P

TOK = 512
UNIT = 8
UNITS = 64
HEADS = 6
WIDTH = 384
STATE = 128
SPAN = 256
FEATURES = 3072
CUT = 96
LANES = 128
EPSILON = 1e-05
F32 = jnp.float32
BF16 = jnp.bfloat16


def dot(a, b, ca=1, cb=0, precision=None):
    return lax.dot_general(
        a, b, (((ca,), (cb,)), ((), ())), precision=precision, preferred_element_type=F32
    )


def iota(shape, dim):
    return lax.broadcasted_iota(jnp.int32, shape, dim)


def indicator(mask, dtype=BF16):
    return jnp.where(mask, 1.0, 0.0).astype(dtype)


def partner_row(route, unit):
    return pl.ds(pl.multiple_of((route[0, unit] >> 6) * UNIT, UNIT), UNIT)


BAND = 128
ALL = slice(0, TOK)
BANDS = [slice(BAND * k, BAND * (k + 1)) for k in range(TOK // BAND)]


def put_band(stage, route, rows, values, first=0):
    for unit in range(rows.start // UNIT, rows.stop // UNIT):
        target, place = partner_row(route, unit), UNIT * unit - rows.start
        for plane in range(values.shape[1] // LANES):
            cols = slice(LANES * plane, LANES * (plane + 1))
            stage[first + plane, target, :] = values[place : place + UNIT, cols]


def sent(stage, planes, rows=slice(0, TOK)):
    return jnp.concatenate([stage[plane, rows, :] for plane in range(planes)], axis=1)


def fill(stage, values):
    for plane in range(values.shape[1] // LANES):
        stage[plane] = values[:, LANES * plane : LANES * (plane + 1)].astype(F32)


def own_band(stage, route, rows, planes):
    units = []
    for unit in range(rows.start // UNIT, rows.stop // UNIT):
        source = partner_row(route, unit)
        parts = [stage[plane, source, :] for plane in range(planes)]
        units.append(jnp.concatenate(parts, axis=1))
    return jnp.concatenate(units, axis=0)


def receive_matrix(index_ref):
    partner = jnp.broadcast_to((index_ref[...] >> 6).astype(F32), (16, UNITS)).astype(BF16)
    repeat = indicator((iota((TOK, UNITS), 0) >> 3) == iota((TOK, UNITS), 1))
    partner = dot(repeat, partner, 1, 1)[:, 0:1].astype(jnp.int32)
    source = partner * UNIT + (iota((TOK, 1), 0) & 7)
    return indicator(iota((TOK, TOK), 1) == source)


def padded_decay(decay_ref):
    decay = decay_ref[...].astype(F32)
    return jnp.concatenate([decay, jnp.zeros((16 - HEADS, TOK), F32)], axis=0).astype(BF16)


def lower_ones():
    return indicator(iota((TOK, TOK), 1) <= iota((TOK, TOK), 0))


def running_of(decay_ref):
    return running_wide(padded_decay(decay_ref), lower_ones())


def running_wide(decay, lower):
    spread = indicator((iota((16, WIDTH), 1) >> 6) == iota((16, WIDTH), 0))
    return dot(lower, dot(decay, spread, 0, 0).astype(BF16))


def rolled(tile, shift):
    return pltpu.roll(tile, shift % LANES, 1)


def cut_state(state):
    low, middle, high = [state[:, LANES * k : LANES * (k + 1)] for k in range(3)]
    lane = iota((STATE, LANES), 1)
    parts = [
        low,
        jnp.where(lane < 32, rolled(low, 32), rolled(middle, 32)),
        jnp.where(lane < 64, rolled(middle, 64), rolled(high, 64)),
        rolled(high, 96),
    ]
    return jnp.concatenate([jnp.where(lane < CUT, part, 0.0) for part in parts], axis=0)


def join_state(slices):
    slices = slices.astype(F32)
    first, second, third, fourth = [slices[STATE * k : STATE * (k + 1)] for k in range(4)]
    lane = iota((STATE, LANES), 1)
    tiles = [
        jnp.where(lane < 96, first, rolled(second, 96)),
        jnp.where(lane < 64, rolled(second, 96), rolled(third, 64)),
        jnp.where(lane < 32, rolled(third, 64), rolled(fourth, 32)),
    ]
    return jnp.concatenate(tiles, axis=1).astype(BF16)


def local_state(keys, values, weight):
    return dot(keys, (values.astype(F32) * weight).astype(BF16), 0, 0)


def three_parts(value):
    high = value.astype(BF16).astype(F32)
    middle = (value - high).astype(BF16).astype(F32)
    return high, middle, value - high - middle


def slice_heads():
    part = lax.axis_index("seq") >> 4
    first = part + (part >> 1)
    return first, first + 1, 64 - 32 * (part & 1)


def link_decays(slices, lane, work):
    column = iota((TOK, LANES), 1)
    held = jnp.where((column >= lane) & (column < lane + 3), slices.astype(F32), 0.0)
    work[0] = jnp.broadcast_to(jnp.sum(held, axis=1, keepdims=True), (TOK, LANES))
    first, second, border = slice_heads()
    wanted = jnp.where(iota((UNITS, LANES), 1) < border, first, second)
    total = jnp.zeros((UNITS, LANES), F32)
    for head in range(HEADS):
        total = jnp.where(wanted == head, work[0, pl.ds(head, UNITS, stride=UNIT), :], total)
    return jnp.exp(total)


def carry(decays, slices, causal):
    slices = jnp.where(iota((TOK, LANES), 1) < CUT, slices.astype(F32), 0.0)
    state = jnp.zeros((UNIT, LANES), F32)
    entering = [state] * UNITS
    for device in range(UNITS) if causal else reversed(range(UNITS)):
        entering[device] = state
        own = slices[UNIT * device : UNIT * (device + 1)]
        state = state * decays[device : device + 1, :] + own
    return jnp.concatenate(entering, axis=0)


def span_rows(index):
    return slice(SPAN * index, SPAN * (index + 1))


def build_inner(rows_ref, cols_ref, decay, lower, inner_ref):
    down = dot(lower, decay, 1, 1)
    across = dot(decay, lower, 1, 1)
    allowed = iota((SPAN, SPAN), 1) <= iota((SPAN, SPAN), 0)
    for index in range(TOK // SPAN):
        span = span_rows(index)
        scores = jnp.where(allowed, dot(rows_ref[span, :], cols_ref[span, :], 1, 1), 0.0)
        for head in range(HEADS):
            spread = down[span, head : head + 1] - across[head : head + 1, span]
            weight = scores * jnp.exp(jnp.minimum(spread, 0.0))
            inner_ref[index, head] = weight.astype(BF16)


def apply_inner(inner_ref, values_ref, keys_ref, queries_ref, running, causal, out_ref):
    lane = iota((SPAN, LANES), 1)
    border = running[SPAN - 1 : SPAN]
    source, target = (0, 1) if causal else (1, 0)
    sign = 1.0 if causal else -1.0
    near = jnp.exp(sign * (border - running[span_rows(source)]))
    state = local_state(keys_ref[span_rows(source), :], values_ref[span_rows(source), :], near)
    far = jnp.exp(sign * (running[span_rows(target)] - border))
    crossing = far * dot(queries_ref[span_rows(target), :], state.astype(BF16))
    side = 1 if causal else 0
    for index in range(TOK // SPAN):
        span = span_rows(index)
        for pair in range(HEADS // 2):
            cols = slice(LANES * pair, LANES * (pair + 1))
            block = values_ref[span, cols]
            nothing = jnp.zeros_like(block)
            total = dot(inner_ref[index, 2 * pair], jnp.where(lane < 64, block, nothing), side, 0)
            total += dot(
                inner_ref[index, 2 * pair + 1], jnp.where(lane < 64, nothing, block), side, 0
            )
            if index == target:
                total += crossing[:, cols]
            out_ref[span, cols] = total.astype(BF16)


def open_raster(x, in_map, out_map, decay_f, decay_r, grad, route, pay, stage):
    lane = iota((UNIT, LANES), 1)
    note = jnp.zeros((UNIT, LANES), F32)
    for place, decay_ref in ((CUT, decay_f), (CUT + 3, decay_r)):
        decay = jnp.concatenate([decay_ref[...].astype(F32), jnp.zeros((2, TOK), F32)], axis=0)
        for offset, part in enumerate(three_parts(jnp.sum(decay, axis=1, keepdims=True))):
            note = jnp.where(lane == place + offset, part, note)
    note = jnp.broadcast_to(note[None], (UNITS, UNIT, LANES)).reshape(TOK, LANES)
    running = running_of(decay_f)
    start = 0
    for source in (in_map, out_map, x, grad):
        put_band(stage, route, ALL, source[...].astype(F32))
        stop = start + source.held.shape[1]
        pay[:, start:stop] = sent(stage, (stop - start) // LANES).astype(BF16)
        if stop >= 640:
            pay.send(cols=slice(0 if stop == 640 else start, stop))
        start = stop
    state = local_state(in_map[...], x[...], jnp.exp(running[TOK - 1 : TOK] - running))
    pay[:, 1024:1152] = (cut_state(state) + note).astype(BF16)
    pay.send(cols=slice(1024, 1152))


def inner_raster(x, in_map, out_map, decay_f, skip, gain, inner, local):
    lower = lower_ones()
    decay = padded_decay(decay_f)
    build_inner(out_map, in_map, decay, lower, inner)
    apply_inner(inner, x, in_map, out_map, running_wide(decay, lower), True, local)


def open_scan(got, decay_r, route, pay, stage):
    slices = got[:, 1024:1152]
    pay[:, 0:128] = carry(link_decays(slices, CUT, stage), slices, True).astype(BF16)
    pay.send(cols=slice(0, 128))
    put_band(stage, route, ALL, jnp.exp(running_of(decay_r)))
    state = local_state(got[:, 0:128], got[:, 256:640], sent(stage, 3))
    pay[:, 128:256] = cut_state(state).astype(BF16)
    pay.send(cols=slice(128, 256))


def inner_scan(
    got, decay_r, route, x, in_map, out_map, grad, inner, local, links_f, links_r, work
):
    take = receive_matrix(route)
    in_map[...] = dot(take, got[:, 0:128]).astype(BF16)
    out_map[...] = dot(take, got[:, 128:256]).astype(BF16)
    x[...] = dot(take, got[:, 256:640]).astype(BF16)
    grad[...] = dot(take, got[:, 640:1024]).astype(BF16)
    lower = lower_ones()
    decay = padded_decay(decay_r)
    build_inner(in_map, out_map, decay, lower, inner)
    apply_inner(inner, x, in_map, out_map, running_wide(decay, lower), False, local)
    slices = got[:, 1024:1152]
    for links, lane in ((links_f, CUT), (links_r, CUT + 3)):
        links[...] = link_decays(slices, lane, work)


def finish_raster(got, out_map, local, decay_f, links, route, pay, stage):
    running = running_of(decay_f)
    entering = join_state(got[:, 0:128])
    pay[:, 384:512] = carry(links, got[:, 128:256], False).astype(BF16)
    for rows in BANDS:
        value = local[rows, :].astype(F32) + jnp.exp(running[rows]) * dot(out_map[rows, :], entering)
        put_band(stage, route, rows, value)
    pay[:, 0:384] = sent(stage, 3).astype(BF16)


def finish_scan(
    got, out_map, local, decay_r, x, grad, skip, gain, route, combined, stats, stage
):
    entering = join_state(got[:, 384:512])
    running = running_of(decay_r)
    weight = jnp.exp(running[TOK - 1 : TOK, :] - running)
    fill(stage, got[:, 0:384])
    y_forward = own_band(stage, route, ALL, 3)
    y_reverse = local[...].astype(F32) + weight * dot(out_map[...], entering)
    total = y_forward + y_reverse + skip[...] * x[...].astype(F32)
    combined[...] = total
    scaled = gain[...] * grad[...].astype(F32)
    squares, inner = token_sums(total * total), token_sums(total * scaled)
    row = iota((UNIT, LANES), 0)
    tile = jnp.zeros((UNIT, LANES), F32)
    for place, sums in ((0, squares), (4, inner)):
        for k in range(4):
            tile = jnp.where(row == place + k, sums[:, LANES * k : LANES * (k + 1)], tile)
    for place in range(8):
        stats[UNIT * place : UNIT * (place + 1), :] = tile


def token_sums(value):
    folded = value[:, 0:128] + value[:, 128:256] + value[:, 256:384]
    ones = jnp.ones((16, LANES), BF16)
    return sum(dot(ones, part.astype(BF16), 1, 1)[0:1] for part in three_parts(folded)[:2])


def gradient(combined, scaled, scale, pull):
    return (scale * scaled - combined * pull).astype(BF16)


def open_back(stats, combined, out_map, grad, gain, decay_r, route, back, pay, stage):
    running = running_of(decay_r)
    tile = jnp.sum(stats[...].reshape(8, 8, LANES), axis=0)
    squares = jnp.concatenate([tile[k : k + 1] for k in range(4)], axis=1)
    inner = jnp.concatenate([tile[k : k + 1] for k in range(4, 8)], axis=1)
    scale = lax.rsqrt(squares / FEATURES + EPSILON)
    pull = scale * scale * scale * inner / FEATURES
    parts = [*three_parts(scale), *three_parts(pull), jnp.zeros((10, TOK), F32)]
    parts = jnp.concatenate(parts, axis=0).astype(BF16)
    row, col = iota((16, 2 * WIDTH), 0), iota((16, 2 * WIDTH), 1)
    both = indicator(((row < 3) & (col < WIDTH)) | ((row >= 3) & (row < 6) & (col >= WIDTH)))
    lanes = indicator(iota((16, LANES), 1) == CUT + iota((16, LANES), 0))
    wide = dot(parts, both, 0, 0)
    put_band(stage, route, ALL, dot(parts, lanes, 0, 0), 3)
    put_band(stage, route, ALL, combined[...])
    pay[:, 0:384] = sent(stage, 3).astype(BF16)
    scaled = gain[...] * grad[...].astype(F32)
    back[...] = gradient(combined[...], scaled, wide[:, 0:WIDTH], wide[:, WIDTH:])
    back.send()
    state = local_state(out_map[...], back[...], jnp.exp(running[TOK - 1 : TOK] - running))
    pay[:, 384:512] = (cut_state(state) + stage[3]).astype(BF16)


def inner_back_scan(decay_r, inner, back, in_map, out_map, local):
    apply_inner(inner, back, out_map, in_map, running_of(decay_r), True, local)


def middle_raster(
    got, out_map, grad, gain, decay_f, links, route, normed, back, pay, stage
):
    running = running_of(decay_f)
    fill(stage, got[...])
    row, col = iota((LANES, 2 * WIDTH), 0) - CUT, iota((LANES, 2 * WIDTH), 1)
    both = indicator(
        ((row >= 0) & (row < 3) & (col < WIDTH)) | ((row >= 3) & (row < 6) & (col >= WIDTH))
    )
    pay[:, 0:128] = carry(links, got[:, 384:512], True).astype(BF16)
    pay.send(cols=slice(0, 128))
    for rows in BANDS:
        moved = own_band(stage, route, rows, 4)
        wide = dot(moved[:, 384:512].astype(BF16), both)
        scale = wide[:, 0:WIDTH]
        total = moved[:, 0:384]
        normed[rows, :] = (total * scale * gain[...]).astype(BF16)
        scaled = gain[...] * grad[rows, :].astype(F32)
        back[rows, :] = gradient(total, scaled, scale, wide[:, WIDTH:])
    normed.send()
    back.send()
    state = local_state(out_map[...], back[...], jnp.exp(running))
    pay[:, 128:256] = cut_state(state).astype(BF16)
    pay.send(cols=slice(128, 256))


def inner_back_raster(decay_f, inner, back, in_map, out_map, skip, local):
    apply_inner(inner, back, out_map, in_map, running_of(decay_f), False, local)
    local[...] = (local[...].astype(F32) + skip[...] * back[...].astype(F32)).astype(BF16)


def finish_back_scan(got, in_map, local, decay_r, links, route, pay, stage):
    running = running_of(decay_r)
    entering = join_state(got[:, 0:128])
    pay[:, 384:512] = carry(links, got[:, 128:256], False).astype(BF16)
    for rows in BANDS:
        value = local[rows, :].astype(F32) + jnp.exp(running[rows]) * dot(in_map[rows, :], entering)
        put_band(stage, route, rows, value)
    pay[:, 0:384] = sent(stage, 3).astype(BF16)


def finish_back_raster(got, in_map, local, decay_f, route, out, stage):
    entering = join_state(got[:, 384:512])
    running = running_of(decay_f)
    last = running[TOK - 1 : TOK, :]
    fill(stage, got[:, 0:384])
    for rows in BANDS:
        carried = jnp.exp(last - running[rows]) * dot(in_map[rows, :], entering)
        total = local[rows, :].astype(F32) + carried + own_band(stage, route, rows, 3)
        out[rows, :] = total.astype(BF16)
        out.send(rows)


class Arriving:
    def __init__(self, source, held, semaphore):
        self.held = held
        self.copy = pltpu.make_async_copy(source, held, semaphore)
        self.copy.start()

    def land(self):
        if self.copy is not None:
            self.copy.wait()
            self.copy = None

    def __getitem__(self, index):
        self.land()
        return self.held[index]


class Leaving:
    def __init__(self, held, target, semaphores):
        self.held, self.target, self.semaphores, self.copies = held, target, semaphores, []

    def __setitem__(self, index, value):
        self.held[index] = value

    def __getitem__(self, index):
        return self.held[index]

    def send(self, rows=None, cols=None):
        held, target = self.held, self.target
        if rows is not None or cols is not None:
            index = (rows or slice(0, TOK), cols or slice(0, held.shape[1]))
            held, target = held.at[index], target.at[index]
        copy = pltpu.make_async_copy(held, target, self.semaphores.at[len(self.copies)])
        copy.start()
        self.copies.append(copy)

    def finish(self):
        if not self.copies:
            self.send()
        for copy in self.copies:
            copy.wait()


def whole_kernel(body, outs, *operands, flops, work=False):
    shapes = [jax.ShapeDtypeStruct(shape, dtype) for shape, dtype in outs]
    size = sum(a.size * a.dtype.itemsize for a in (*operands, *shapes))
    return pl.pallas_call(
        body,
        out_shape=shapes,
        scratch_shapes=[pltpu.VMEM((1, TOK, LANES), F32)] * work,
        compiler_params=pltpu.CompilerParams(vmem_limit_bytes=60 * 2**20),
        cost_estimate=pl.CostEstimate(flops=flops, bytes_accessed=size, transcendentals=0),
        name=body.__name__,
    )(*operands)


def kernel(body, outs, *operands, arrived=0, stage=0, after=(), flops=400_000_000):
    shapes = [jax.ShapeDtypeStruct(*out[:2]) for out in outs]
    size = sum(a.size * a.dtype.itemsize for a in (*operands, *shapes))
    sends = [(*out, 1)[2] for out in outs]
    count = len(operands)
    own = [
        place >= arrived and (not arrived or a.dtype == jnp.int32 or a.size > 5_000)
        for place, a in enumerate(operands)
    ]

    def wrapped(*refs):
        sources, refs = refs[:count], refs[count + len(after) :]
        targets, scratch = refs[: len(outs)], iter(refs[len(outs) :])
        held = [(next(scratch), next(scratch)) if mine else None for mine in own]
        given = list(sources)
        for place in sorted(range(count), key=lambda k: operands[k].size):
            if own[place]:
                given[place] = Arriving(sources[place], *held[place])
        results = [
            Leaving(next(scratch), target, next(scratch)) if times else target
            for target, times in zip(targets, sends, strict=True)
        ]
        body(*given, *results, *([next(scratch)] if stage else []))
        for operand in given:
            if isinstance(operand, Arriving):
                operand.land()
        for result in results:
            if isinstance(result, Leaving):
                result.finish()

    scratch_shapes = []
    for operand, mine in zip(operands, own, strict=True):
        if mine:
            space = pltpu.SMEM if operand.dtype == jnp.int32 else pltpu.VMEM
            scratch_shapes += [space(operand.shape, operand.dtype), pltpu.SemaphoreType.DMA]
    for shape, times in zip(shapes, sends, strict=True):
        if times:
            scratch_shapes += [pltpu.VMEM(shape.shape, shape.dtype), pltpu.SemaphoreType.DMA((times,))]
    if stage:
        scratch_shapes.append(pltpu.VMEM((stage // LANES, TOK, LANES), F32))
    whole = pl.BlockSpec(memory_space=pltpu.VMEM)
    apart = pl.BlockSpec(memory_space=pl.ANY)
    operands = [
        pltpu.with_memory_space_constraint(a, pltpu.HBM) if mine else a
        for a, mine in zip(operands, own, strict=True)
    ]
    return pl.pallas_call(
        wrapped,
        out_shape=[
            pltpu.HBM(shape.shape, shape.dtype) if times else shape
            for shape, times in zip(shapes, sends, strict=True)
        ],
        in_specs=[apart if mine else whole for mine in own] + [apart] * len(after),
        out_specs=[apart if times else whole for times in sends],
        scratch_shapes=scratch_shapes,
        compiler_params=pltpu.CompilerParams(vmem_limit_bytes=48 * 2**20),
        cost_estimate=pl.CostEstimate(flops=flops, bytes_accessed=size, transcendentals=0),
        name=body.__name__,
    )(*operands, *(pltpu.with_memory_space_constraint(a, pltpu.HBM) for a in after))


def exchange(pay):
    return lax.all_to_all(pay, "seq", split_axis=0, concat_axis=0, tiled=True)


def shards(
    ssm_input,
    input_map,
    output_map,
    decay_forward,
    decay_reverse,
    skip_gain,
    norm_gain,
    scan_order,
    raster_order,
    grad_normed,
):
    to_scan = raster_order.reshape(1, UNITS)
    to_raster = scan_order.reshape(1, UNITS)
    skip = jnp.repeat(skip_gain, WIDTH // HEADS).reshape(1, WIDTH)
    gain = norm_gain.reshape(1, WIDTH)
    wide16, wide32 = ((TOK, WIDTH), BF16), ((TOK, WIDTH), F32)
    rows16 = ((TOK, STATE), BF16)
    inner16 = ((TOK // SPAN, HEADS, SPAN, SPAN), BF16)

    def pay(lanes, sends=2):
        return ((TOK, lanes), BF16, sends)

    (pay1,) = kernel(
        open_raster, [pay(1152, 3)],
        ssm_input, input_map, output_map, decay_forward, decay_reverse, grad_normed, to_scan,
        stage=384,
    )
    got1 = exchange(pay1)
    inner_f, local_f = whole_kernel(
        inner_raster, [inner16, wide16],
        ssm_input, input_map, output_map, decay_forward, skip, gain, flops=8_000_000_000,
    )
    (pay2,) = kernel(
        open_scan, [pay(256)], got1, decay_reverse, to_raster, arrived=1, stage=384,
    )
    got2 = exchange(pay2)
    links32 = ((UNITS, LANES), F32)
    x_scan, in_scan, out_scan, grad_scan, inner_r, local_r, links_f, links_r = whole_kernel(
        inner_scan, [wide16, rows16, rows16, wide16, inner16, wide16, links32, links32],
        got1, decay_reverse, to_raster, flops=8_000_000_000, work=True,
    )
    (pay3,) = kernel(
        finish_raster, [pay(512, 0)],
        got2, output_map, local_f, decay_forward, links_r, to_scan, arrived=1, stage=384,
    )
    got3 = exchange(pay3)
    combined, stats = kernel(
        finish_scan, [(*wide32, 0), ((64, LANES), F32, 0)],
        got3, out_scan, local_r, decay_reverse, x_scan, grad_scan, skip, gain, to_raster, arrived=1, stage=384,
    )
    all_stats = lax.all_to_all(stats, "head", split_axis=0, concat_axis=0, tiled=True)
    back_scan, pay4 = kernel(
        open_back, [wide16, pay(512, 0)],
        all_stats, combined, out_scan, grad_scan, gain, decay_reverse, to_raster, arrived=2, stage=512,
    )
    got4 = exchange(pay4)
    (local_br,) = kernel(
        inner_back_scan, [wide16], decay_reverse, inner_r, back_scan, in_scan, out_scan,
        arrived=1, flops=4_000_000_000,
    )
    normed, back, pay5 = kernel(
        middle_raster, [wide16, wide16, pay(256)],
        got4, output_map, grad_normed, gain, decay_forward, links_r,
        to_scan, arrived=1, stage=512,
    )
    got5 = exchange(pay5)
    (local_bf,) = kernel(
        inner_back_raster, [wide16],
        decay_forward, inner_f, back, input_map, output_map, skip, arrived=1, flops=4_000_000_000,
    )
    (pay6,) = kernel(
        finish_back_scan, [pay(512, 0)],
        got5, in_scan, local_br, decay_reverse, links_f, to_raster, arrived=1, stage=384,
        after=(local_bf,),
    )
    got6 = exchange(pay6)
    (grad_input,) = kernel(
        finish_back_raster, [(*wide16, 4)],
        got6, input_map, local_bf, decay_forward, to_scan, arrived=1, stage=384,
    )
    return normed, grad_input


def solution(mesh):
    return jax.shard_map(
        shards,
        mesh=mesh,
        in_specs=(
            P("seq", "head"),
            P("seq", "head"),
            P("seq", "head"),
            P("head", "seq"),
            P("head", "seq"),
            P("head"),
            P("head"),
            P("seq"),
            P("seq"),
            P("seq", "head"),
        ),
        out_specs=(P("seq", "head"), P("seq", "head")),
        check_vma=False,
    )
```
